512 devices in a mesh: section: 16 (over x, y), expert: 32 (over z, core).
Axes of the slice: x: 4, y: 4, z: 16, core: 2. Of those that a mesh axis runs over, the one named last changes fastest.
Arguments:
- activations: bfloat16 [16, 4096, 2048], P('section', 'expert'), may hold values from -60 to 60
- cotangents: bfloat16 [16, 4096, 2048], P('section', 'expert'), may hold values from -6 to 6
- norm_gain: bfloat16 [16, 2048], P('section'), may hold values from 0.25 to 1.75
- routes: int32 [16, 4096, 2], P('section', 'expert'), may hold values from 0 to 15, all different within a row; in each aligned block of 128 rows (0 to 127, 128 to 255, ..., all dimensions but the last counted through in order) at most 24 rows name the same one
- lengths: int32 [16, 32], P('section', 'expert'), may hold values from 64 to 128, as said below
- router_weight: bfloat16 [16, 2048, 16], P('section'), may hold values from -0.125 to 0.125
- gate_weight: bfloat16 [16, 32, 2048, 256], P('section', 'expert'), may hold values from -0.125 to 0.125
- up_weight: bfloat16 [16, 32, 2048, 256], P('section', 'expert'), may hold values from -0.125 to 0.125
- down_weight: bfloat16 [16, 32, 256, 2048], P('section', 'expert'), may hold values from -0.25 to 0.25
Outputs:
- layer_input_gradient: bfloat16 [16, 4096, 2048], P('section', 'expert')
- router_grad: float32 [16, 2048, 16], P('section')
- norm_gain_gradient: float32 [16, 2048], P('section')
The draws below stay inside these ranges and needn't reach their ends.
Inputs may be any that keep to these rules, and one draw needn't show every extreme that they name: `routes`: each row names 2 different experts; among the rows of one device, padding rows included, no expert is named more than 24 times, a bound that some block reaches there in every draw. The first lengths[s, b] rows of each device's block are live, the rest are padding; some device's block is full in every draw.
All inputs are finite; a program needn't handle non-finite values.
Results may differ from the reference program's by a relative error of at most 0.03.
Values may be sent and summed in bfloat16 or wider, within the bound.
A program may use at most 128 MiB of HBM per device.

```python
import math
import jax
import jax.numpy as jnp
import numpy as np
from jax import lax

D = 2048
H = 512
TOP = 2
ROWS = 128
HALF = 256
EXPERTS = 16
CAP = 24
TOKENS = 4096
N_SECTION = 16
N_EXPERT = 32


def draw_activations(key, part):
    first, second, third = jax.random.split(key, 3)
    base = jnp.clip(jax.random.normal(first, (N_SECTION, TOKENS, D), jnp.float32), -4.0, 4.0)
    row_scale = jnp.exp(jax.random.uniform(second, (N_SECTION, TOKENS, 1), jnp.float32, math.log(0.3), math.log(3.0)))
    column_scale = jnp.exp(jax.random.uniform(third, (N_SECTION, 1, D), jnp.float32, math.log(0.3), math.log(3.0)))
    return jnp.clip(base * row_scale * column_scale, -60.0, 60.0).astype(jnp.bfloat16)


def draw_lengths(key, part):
    first, second = jax.random.split(key, 2)
    counts = jax.random.randint(first, (N_SECTION * N_EXPERT,), ROWS // 2, ROWS + 1, jnp.int32)
    full_block = jax.random.randint(second, (), 0, N_SECTION * N_EXPERT, jnp.int32)
    counts = counts.at[full_block].set(ROWS)
    return counts.reshape(N_SECTION, N_EXPERT).astype(jnp.int32)


def levels(own_key, shape, cuts, low, largest):
    factor_of, own = 1.0, jax.random.fold_in(own_key, 6)
    for dim, blocks in cuts:
        steps = jnp.exp(jax.random.uniform(jax.random.fold_in(own, dim), (blocks,), jnp.float32, low / len(cuts), largest / len(cuts)))
        factor_of = factor_of * jnp.repeat(steps, shape[dim] // blocks).reshape([-1 if axis == dim else 1 for axis in range(len(shape))])
    return factor_of


def shared_out(key, own, number, rows, number_of, top, bound, skew):
    sequence = jax.random.permutation(key, number_of)
    heavy_load, common = portions_of(number_of, rows * top, bound, skew, True), portions_of(number_of, rows * top, bound, skew, False)
    places = jnp.arange(number_of)

    def named(sizes, rotation):
        used = int((sizes > 0).sum())
        fixed = max(1, used // 4)
        moved = fixed + (places - fixed + rotation * (used - fixed)) % max(1, number_of - fixed)
        return jnp.zeros((number_of,), jnp.int32).at[sequence[jnp.where(places < fixed, places, moved)]].set(jnp.asarray(sizes, jnp.int32))

    sizes = jnp.where(number % 4 == 0, named(heavy_load, number // 4), named(common, number - number // 4 - 1))
    mixed = jax.random.permutation(jax.random.fold_in(own, 3), number_of)
    source_of, sink = mixed[0:number_of // 2 * 2:2], mixed[1:number_of // 2 * 2:2]
    room = jnp.minimum(sizes[source_of] - 1, bound - sizes[sink]) // 2
    room = jnp.where((source_of == sequence[0]) | (sink == sequence[0]) | (sizes[sink] == 0), 0, jnp.maximum(room, 0))
    moved = jax.random.randint(jax.random.fold_in(own, 4), (number_of // 2,), 0, 1 << 20) % (room + 1)
    sizes = sizes.at[source_of].add(-moved).at[sink].add(moved)
    members = jnp.searchsorted(jnp.cumsum(sizes), jnp.arange(rows * top), side="right").astype(jnp.int32)
    grid = members.reshape(top, rows).T
    grid = grid[jax.random.permutation(jax.random.fold_in(own, 1), rows)]
    rotation = jax.random.randint(jax.random.fold_in(own, 2), (rows, 1), 0, top)
    return jnp.take_along_axis(grid, (jnp.arange(top)[None, :] + rotation) % top, axis=1)


def portions_of(amount, total, bound, slope, full):
    portions = [(1 << 20) // math.isqrt(rank ** slope) + 1 for rank in range(1, amount + 1)]
    largest = bound if full else min(bound, max(-(-total // amount), total * portions[0] // sum(portions)))
    least = 1 if total - largest >= amount - 1 else 0
    holding, spare = [largest] + [least] * (amount - 1), total - largest - least * (amount - 1)
    while spare > 0:
        movable = [i for i in range(1, amount) if holding[i] < largest] or [i for i in range(1, amount) if holding[i] < bound]
        pool, remaining = sum([portions[i] for i in movable]), spare
        for i in movable:
            addition = min(bound - holding[i], max(1, remaining * portions[i] // pool), spare)
            holding[i] = holding[i] + addition
            spare = spare - addition
    return np.array(holding)


def gaussian(stream_key, dims, deviation, bound, pieces=(), kind=jnp.bfloat16):
    drawn = deviation * jax.random.normal(stream_key, dims, jnp.float32)
    if pieces:
        drawn = drawn * levels(stream_key, dims, pieces, -0.22, 0.18)
    return jnp.clip(drawn, -bound, bound).astype(kind)


def setup_inputs(seed: int = 0) -> dict:
    key_list = jax.random.split(jax.random.key(seed), 10)
    activations = draw_activations(jax.random.fold_in(key_list[9], 71), 0)
    cotangents = gaussian(key_list[1], (N_SECTION, TOKENS, D), 1.0, 6.0, ((0, 16), (1, 32)))
    norm_gain = jnp.clip(1.0 + 0.15 * jax.random.normal(key_list[2], (N_SECTION, D), jnp.float32), 0.25, 1.75).astype(jnp.bfloat16)
    routes_keys = jax.random.split(jax.random.fold_in(key_list[3], 1), N_SECTION * TOKENS // ROWS)
    routes_turns = jax.random.permutation(jax.random.fold_in(key_list[3], 3), N_SECTION * TOKENS // ROWS)
    routes = jax.vmap(lambda own, number: shared_out(jax.random.fold_in(key_list[3], 2), own, number, ROWS, EXPERTS, TOP, CAP, 2))(routes_keys, routes_turns).reshape((N_SECTION, TOKENS, TOP))
    lengths = draw_lengths(jax.random.fold_in(key_list[9], 71), 0)
    router_weight = gaussian(key_list[5], (N_SECTION, D, EXPERTS), D ** -0.5, 0.125, ((0, 16),))
    gate_weight = gaussian(key_list[6], (N_SECTION, N_EXPERT, D, HALF), D ** -0.5, 0.125, ((0, 16), (1, 32)))
    up_weight = gaussian(key_list[7], (N_SECTION, N_EXPERT, D, HALF), D ** -0.5, 0.125, ((0, 16), (1, 32)))
    down_weight = gaussian(key_list[8], (N_SECTION, N_EXPERT, HALF, D), H ** -0.5, 0.25, ((0, 16), (1, 32)))
    return dict(activations=activations, cotangents=cotangents, norm_gain=norm_gain, routes=routes, lengths=lengths, router_weight=router_weight, gate_weight=gate_weight, up_weight=up_weight, down_weight=down_weight)


EPSILON = 1e-05

def expert_pass(rows_in, grad_rows, gate_pair, up_pair, down_pair):
    out_total = jnp.zeros(rows_in.shape, jnp.float32)
    back_total = jnp.zeros(rows_in.shape, jnp.float32)
    for which_half in range(2):
        gate_pre = jnp.dot(rows_in, gate_pair[which_half], preferred_element_type=jnp.float32)
        up_pre = jnp.dot(rows_in, up_pair[which_half], preferred_element_type=jnp.float32)
        logistic = jax.nn.sigmoid(gate_pre)
        hidden = (gate_pre * logistic * up_pre).astype(jnp.bfloat16)
        expert_out = jnp.dot(hidden, down_pair[which_half], preferred_element_type=jnp.float32).astype(jnp.bfloat16)
        hidden_grad = jnp.dot(grad_rows, down_pair[which_half].T, preferred_element_type=jnp.float32)
        gate_grad = (hidden_grad * up_pre * logistic * (1.0 + gate_pre * (1.0 - logistic))).astype(jnp.bfloat16)
        up_grad = (hidden_grad * gate_pre * logistic).astype(jnp.bfloat16)
        expert_back = jnp.dot(gate_grad, gate_pair[which_half].T, preferred_element_type=jnp.float32)
        expert_back = expert_back + jnp.dot(up_grad, up_pair[which_half].T, preferred_element_type=jnp.float32)
        out_total = out_total + expert_out.astype(jnp.float32)
        back_total = back_total + expert_back.astype(jnp.bfloat16).astype(jnp.float32)
    return (out_total, back_total)

def one_section(arriving, returned_cotangents, gain, picks, counts, router, gate_all, up_all, down_all):
    token_count = arriving.shape[0]
    complete_input = arriving.astype(jnp.float32)
    mean_sq = lax.optimization_barrier(jnp.mean(complete_input * complete_input, axis=-1, keepdims=True))
    inverse_root_mean = lax.rsqrt(mean_sq + EPSILON)
    unit_input = complete_input * inverse_root_mean
    gain_broadcast = gain.astype(jnp.float32)
    normalized_rows = (unit_input * gain_broadcast).astype(jnp.bfloat16)
    logits = jnp.dot(normalized_rows, router, preferred_element_type=jnp.float32)
    chosen = jnp.take_along_axis(logits, picks, axis=1)
    gates = 1.0 / lax.optimization_barrier(jnp.sum(jnp.exp(chosen[:, None, :] - chosen[:, :, None]), axis=2))
    position = jnp.arange(token_count, dtype=jnp.int32)
    live = position % ROWS < counts[position // ROWS]
    pair_ids = picks.reshape(-1)
    pair_live = jnp.repeat(live, TOP)
    expert_ids = jnp.arange(EXPERTS, dtype=jnp.int32)
    hot = ((pair_ids[:, None] == expert_ids[None, :]) & pair_live[:, None]).astype(jnp.int32)
    place_index = lax.optimization_barrier(jnp.sum((jnp.cumsum(hot, axis=0) - hot) * hot, axis=1))
    per_expert = N_EXPERT * CAP
    target = jnp.where(pair_live, pair_ids * per_expert + place_index, EXPERTS * per_expert).astype(jnp.int32)
    owner = jnp.repeat(position, TOP).astype(jnp.int32)
    table = jnp.full((EXPERTS * per_expert + 1,), token_count, jnp.int32).at[target].set(owner)
    table = table[:-1].reshape(EXPERTS, per_expert)
    padded_rows = jnp.concatenate([normalized_rows, jnp.zeros((1, D), jnp.bfloat16)], axis=0)
    padded_grads = jnp.concatenate([returned_cotangents, jnp.zeros((1, D), jnp.bfloat16)], axis=0)

    def per_expert_work(payload):
        index_rows, gate_pair, up_pair, down_pair = payload
        return expert_pass(padded_rows[index_rows], padded_grads[index_rows], gate_pair, up_pair, down_pair)
    outs, backs = lax.map(per_expert_work, (table, gate_all.reshape(EXPERTS, 2, D, HALF), up_all.reshape(EXPERTS, 2, D, HALF), down_all.reshape(EXPERTS, 2, HALF, D)))
    flat_out = outs.reshape(EXPERTS * per_expert, D)
    flat_back = backs.reshape(EXPERTS * per_expert, D)
    safe = jnp.minimum(target, EXPERTS * per_expert - 1)
    valid = pair_live.astype(jnp.float32)[:, None]
    out_pairs = (flat_out[safe] * valid).reshape(token_count, TOP, D)
    back_pairs = (flat_back[safe] * valid).reshape(token_count, TOP, D)
    gate_share = lax.optimization_barrier(jnp.sum(out_pairs * returned_cotangents.astype(jnp.float32)[:, None, :], axis=-1))
    moe_grad = lax.optimization_barrier(jnp.sum(back_pairs * gates[:, :, None], axis=1))
    select_grad = gates * (gate_share - lax.optimization_barrier(jnp.sum(gates * gate_share, axis=-1, keepdims=True)))
    onehot = (picks[:, :, None] == expert_ids[None, None, :]).astype(jnp.float32)
    logit_grad = jnp.einsum('rke,rk->re', onehot, select_grad)
    normalized_gradient = moe_grad + jnp.dot(logit_grad, router.astype(jnp.float32).T, precision=lax.Precision.HIGHEST)
    router_grad = jnp.dot(normalized_rows.astype(jnp.float32).T, logit_grad, precision=lax.Precision.HIGHEST)
    norm_gain_gradient = lax.optimization_barrier(jnp.sum(normalized_gradient * unit_input, axis=0))
    gain_scaled_rows = normalized_gradient * gain_broadcast
    layer_input_gradient = returned_cotangents.astype(jnp.float32) + inverse_root_mean * (gain_scaled_rows - unit_input * lax.optimization_barrier(jnp.mean(gain_scaled_rows * unit_input, axis=-1, keepdims=True)))
    return (layer_input_gradient.astype(jnp.bfloat16), router_grad, norm_gain_gradient)

def reference(activations, cotangents, norm_gain, routes, lengths, router_weight, gate_weight, up_weight, down_weight):
    arriving = jnp.roll(activations, 1, axis=0)
    returned_cotangents = jnp.roll(cotangents, -1, axis=0)

    def section_work(payload):
        return one_section(*payload)
    layer_input_gradient, router_grad, norm_gain_gradient = lax.map(section_work, (arriving, returned_cotangents, norm_gain, routes, lengths, router_weight, gate_weight, up_weight, down_weight))
    return (layer_input_gradient, router_grad, norm_gain_gradient)
```

```python
import functools

import jax
import jax.numpy as jnp
from jax import lax
from jax.experimental import pallas as pl
from jax.experimental.pallas import tpu as pltpu
from jax.sharding import PartitionSpec as P

EPSILON = 1e-05
LANES = 128
MESH = pl.DeviceIdType.MESH
F32 = jnp.float32
BF16 = jnp.bfloat16


def from_behind(value, axis, steps):
    count = lax.axis_size(axis)
    pairs = [(source, (source + steps) % count) for source in range(count)]
    return lax.ppermute(value, axis, pairs)


def dot(a, b, contract=(1, 0)):
    return lax.dot_general(
        a, b, (((contract[0],), (contract[1],)), ((), ())), preferred_element_type=F32
    )


def split(value):
    high = value.astype(BF16)
    return high, (value - high.astype(F32)).astype(BF16)


def kernel(
    nz,
    cap,
    disp,
    normed,
    arriving,
    returned,
    inv,
    gain,
    picks,
    targets,
    gates,
    router_t,
    gate_hbm,
    up_hbm,
    down_hbm,
    lig,
    totals,
    gate_w,
    up_w,
    down_w,
    buf,
    own,
    psend,
    precv,
    own_share,
    share_send,
    share_recv,
    rsend,
    ret,
    ssend,
    sret,
    weights,
    stage,
    q_src,
    q_dst,
    x_src,
    x_dst,
    a_src,
    a_dst,
    w_sem,
    l_sem,
    d_send,
    d_recv,
    f_send,
    f_recv,
    p_send,
    p_recv,
    h_send,
    h_recv,
    r_send,
    r_recv,
    s_send,
    s_recv,
    q_send,
    q_recv,
    x_send,
    x_recv,
    a_send,
    a_recv,
):
    steps = nz // 2
    half_width = gate_w.shape[1]
    width = gate_w.shape[0]
    half_model = width // 2
    rows = normed.shape[0]
    section = lax.axis_index("section")
    me = lax.axis_index("expert")
    chip = me // 2
    core = me - chip * 2
    sibling = chip * 2 + 1 - core

    def at_offset(offset):
        return lax.rem(chip + offset + nz, nz) * 2 + core

    def remote(src, dst, send, recv, target):
        return pltpu.make_async_remote_copy(
            src_ref=src,
            dst_ref=dst,
            send_sem=send,
            recv_sem=recv,
            device_id=(section, target),
            device_id_type=MESH,
        )

    def offset_of(step, side):
        if side == 0:
            return steps - step
        return lax.rem(steps + step, nz) if not isinstance(step, int) else (steps + step) % nz

    def dispatch(step, side):
        offset = offset_of(step, side)
        target = at_offset(offset)
        return remote(
            disp.at[target // 2],
            buf.at[step, side],
            d_send.at[step, side],
            d_recv.at[step, side],
            target,
        )

    def forward(step, side):
        return remote(
            buf.at[step, side],
            buf.at[step, 2 + side],
            f_send.at[step, side],
            f_recv.at[step, side],
            sibling,
        )

    def partial(step):
        return remote(psend.at[step], precv.at[step], p_send.at[step], p_recv.at[step], sibling)

    def partial_share(step):
        return remote(
            share_send.at[step], share_recv.at[step], h_send.at[step], h_recv.at[step], sibling
        )

    def give_back(step, side):
        target = at_offset(-offset_of(step, side))
        return remote(
            rsend.at[step, side],
            ret.at[chip],
            r_send.at[step, side],
            r_recv.at[step, side],
            target,
        )

    def give_share(step, side):
        target = at_offset(-offset_of(step, side))
        return remote(
            ssend.at[step, side],
            sret.at[chip],
            s_send.at[step, side],
            s_recv.at[step, side],
            target,
        )

    barrier = pltpu.get_barrier_semaphore()

    def greet(offset, carry):
        pl.semaphore_signal(
            barrier, inc=1, device_id=(section, at_offset(offset)), device_id_type=MESH
        )
        return carry

    lax.fori_loop(1, nz, greet, 0)
    pl.semaphore_signal(barrier, inc=1, device_id=(section, sibling), device_id_type=MESH)
    pl.semaphore_wait(barrier, nz)

    def send_both(step, carry):
        dispatch(step, 0).start()

        @pl.when(step > 0)
        def _():
            dispatch(step, 1).start()

        return carry

    lax.fori_loop(0, steps, send_both, 0)
    self_copy = pltpu.make_async_copy(disp.at[chip], buf.at[0, 1], l_sem.at[0])
    self_copy.start()
    loads = [
        pltpu.make_async_copy(gate_hbm, gate_w, w_sem.at[0]),
        pltpu.make_async_copy(up_hbm, up_w, w_sem.at[1]),
        pltpu.make_async_copy(down_hbm, down_w, w_sem.at[2]),
    ]
    for load in loads:
        load.start()

    slots = lax.broadcasted_iota(jnp.int32, (rows, nz * 2 * cap), 1)
    for part in range(2):
        mix = jnp.where(slots == targets[:, 0:1] + part * cap, gates[:, 0:1], 0.0)
        mix = mix + jnp.where(slots == targets[:, 1:2] + part * cap, gates[:, 1:2], 0.0)
        high, low = split(mix)
        weights[part, 0:rows, :] = high
        weights[part, rows : 2 * rows, :] = low
    stage[...] = jnp.zeros_like(stage)

    self_copy.wait()
    for load in loads:
        load.wait()

    def receive(step):
        for side in range(2):
            if side == 0:
                dispatch(step, side).wait_recv()
            else:

                @pl.when(step > 0)
                def _():
                    dispatch(step, 1).wait_recv()

            forward(step, side).start()

    def compute(step):
        for side in range(2):
            forward(step, side).wait_recv()
        block = buf[step].reshape(8 * cap, width)

        def part(value, which):
            return value.reshape(4, 2 * cap, half_width)[:, which * cap : (which + 1) * cap].reshape(
                4 * cap, half_width
            )

        gate_pre = part(dot(block, gate_w[...]), 0)
        up_pre = part(dot(block, up_w[...]), 0)
        hidden_grad = part(dot(block, down_w[...], (1, 1)), 1)
        logistic = jax.nn.sigmoid(gate_pre)
        activated = gate_pre * logistic
        share = jnp.sum(activated * up_pre * hidden_grad, axis=1, keepdims=True)
        diagonal = lax.broadcasted_iota(jnp.int32, (cap, LANES), 0) == lax.broadcasted_iota(
            jnp.int32, (cap, LANES), 1
        )
        for which in range(4):
            column = share[which * cap : (which + 1) * cap]
            line = jnp.sum(jnp.where(diagonal, column, 0.0), axis=0, keepdims=True)
            tile = jnp.broadcast_to(line, (8, LANES))
            if which < 2:
                own_share[step, which] = tile
            else:
                share_send[step, which - 2] = tile
        partial_share(step).start()
        gate_grad = (
            hidden_grad * up_pre * logistic * (1.0 + gate_pre * (1.0 - logistic))
        ).astype(BF16)
        up_grad = (hidden_grad * activated).astype(BF16)
        chunk = min(512, width)
        for start in range(0, width, chunk):
            columns = slice(start, start + chunk)
            back = dot(gate_grad, gate_w[columns, :], (1, 1)) + dot(
                up_grad, up_w[columns, :], (1, 1)
            )
            own[step, :, columns] = back[: 2 * cap]
            psend[step, :, columns] = back[2 * cap :].astype(BF16)
        partial(step).start()

    def finish(step):
        partial_share(step).wait_recv()
        for side in range(2):
            ssend[step, side] = own_share[step, side] + share_recv[step, side]
        partial(step).wait_recv()
        total = own[step] + precv[step].astype(F32)
        for side in range(2):
            mine = total[side * cap : (side + 1) * cap]
            stacked = jnp.concatenate([mine[:, :half_model], mine[:, half_model:]], axis=0)
            rsend[step, side] = stacked.astype(BF16)
        for side in range(2):
            if side == 0:
                give_share(step, side).start()
                give_back(step, side).start()
            else:

                @pl.when(step > 0)
                def _():
                    give_share(step, 1).start()
                    give_back(step, 1).start()

    def pipeline(turn, carry):
        @pl.when(turn < steps)
        def _():
            receive(turn)

        @pl.when((turn >= 1) & (turn <= steps))
        def _():
            compute(turn - 1)

        @pl.when(turn >= 2)
        def _():
            finish(turn - 2)

        return carry

    lax.fori_loop(0, steps + 2, pipeline, 0)
    self_back = pltpu.make_async_copy(rsend.at[0, 1], ret.at[chip], l_sem.at[1])
    self_share = pltpu.make_async_copy(ssend.at[0, 1], sret.at[chip], l_sem.at[2])
    self_back.start()
    self_share.start()
    self_back.wait()
    self_share.wait()

    def wait_share(step, carry):
        give_share(step, 0).wait_recv()

        @pl.when(step > 0)
        def _():
            give_share(step, 1).wait_recv()

        return carry

    lax.fori_loop(0, steps, wait_share, 0)
    shares = jnp.max(sret[...], axis=1)
    expert_ids = lax.broadcasted_iota(jnp.int32, (rows, nz), 1)
    places = lax.broadcasted_iota(jnp.int32, (rows, LANES), 1)
    share_parts = split(shares)
    share_parts = share_parts + ((shares - share_parts[0].astype(F32) - share_parts[1].astype(F32)).astype(BF16),)
    gate_share = []
    for k in range(2):
        pick = picks[:, k : k + 1]
        onehot = (expert_ids == pick).astype(BF16)
        line = dot(onehot, share_parts[0]) + dot(onehot, share_parts[1]) + dot(onehot, share_parts[2])
        place = targets[:, k : k + 1] - pick * (2 * cap)
        gate_share.append(
            jnp.sum(jnp.where(places == place, line, 0.0), axis=1, keepdims=True)
        )
    mean_share = gates[:, 0:1] * gate_share[0] + gates[:, 1:2] * gate_share[1]
    logit_grad = jnp.zeros((rows, nz), F32)
    for k in range(2):
        select_grad = gates[:, k : k + 1] * (gate_share[k] - mean_share)
        logit_grad = logit_grad + jnp.where(expert_ids == picks[:, k : k + 1], select_grad, 0.0)
    grad_high, grad_low = split(logit_grad)
    router_part = dot(grad_high, router_t[...]) + dot(grad_low, router_t[...])
    router_term = dot(grad_high, normed[...], (0, 0)) + dot(grad_low, normed[...], (0, 0))
    blocks = width // LANES
    for block in range(blocks):
        stage[:, block, :] = router_term[:, block * LANES : (block + 1) * LANES]

    def wait_back(step, carry):
        give_back(step, 0).wait_recv()

        @pl.when(step > 0)
        def _():
            give_back(step, 1).wait_recv()

        return carry

    lax.fori_loop(0, steps, wait_back, 0)
    came_back = ret[...].reshape(nz * 2 * cap, half_model)
    moved = []
    for part in range(2):
        both = dot(weights[part], came_back)
        moved.append(both[:rows] + both[rows:])
    normed_grad = jnp.concatenate(moved, axis=1) + router_part
    unit = arriving[...].astype(F32) * inv[...]
    gain_term = jnp.sum(normed_grad * unit, axis=0, keepdims=True)
    for block in range(nz):
        stage[block, blocks : blocks + 1, :] = gain_term[:, block * LANES : (block + 1) * LANES]
    q_src[...] = stage[...].astype(BF16)

    def reduce_copy(offset):
        target = at_offset(offset)
        return remote(
            q_src.at[target // 2], q_dst.at[offset], q_send.at[offset], q_recv.at[offset], target
        )

    def gather_copy(offset):
        return remote(
            a_src, a_dst.at[chip], a_send.at[offset], a_recv.at[offset], at_offset(offset)
        )

    def start_reduce(offset, carry):
        reduce_copy(offset).start()
        return carry

    lax.fori_loop(1, nz, start_reduce, 0)
    self_reduce = pltpu.make_async_copy(q_src.at[chip], q_dst.at[0], l_sem.at[3])
    self_reduce.start()

    scaled = normed_grad * gain[...].astype(F32)
    mean_scaled = jnp.mean(scaled * unit, axis=-1, keepdims=True)
    lig[...] = (returned[...].astype(F32) + inv[...] * (scaled - unit * mean_scaled)).astype(BF16)

    def wait_reduce(offset, carry):
        reduce_copy(offset).wait_recv()
        return carry

    self_reduce.wait()
    lax.fori_loop(1, nz, wait_reduce, 0)
    x_src[...] = jnp.sum(q_dst[...].astype(F32), axis=0)
    across = remote(x_src, x_dst, x_send.at[0], x_recv.at[0], sibling)
    across.start()
    across.wait_recv()
    a_src[...] = (x_src[...] + x_dst[...]).astype(BF16)

    def start_gather(offset, carry):
        gather_copy(offset).start()
        return carry

    lax.fori_loop(1, nz, start_gather, 0)
    self_gather = pltpu.make_async_copy(a_src, a_dst.at[chip], l_sem.at[4])
    self_gather.start()
    self_gather.wait()

    def drain(step, carry):
        dispatch(step, 0).wait_send()
        forward(step, 0).wait_send()
        forward(step, 1).wait_send()
        partial(step).wait_send()
        partial_share(step).wait_send()
        give_back(step, 0).wait_send()
        give_share(step, 0).wait_send()

        @pl.when(step > 0)
        def _():
            dispatch(step, 1).wait_send()
            give_back(step, 1).wait_send()
            give_share(step, 1).wait_send()

        return carry

    lax.fori_loop(0, steps, drain, 0)
    across.wait_send()

    def wait_gather(offset, carry):
        reduce_copy(offset).wait_send()
        gather_copy(offset).wait()
        return carry

    lax.fori_loop(1, nz, wait_gather, 0)
    totals[...] = a_dst[...].astype(F32)


def exchange(
    nz, cap, disp, normed, arriving, returned, inv, gain, picks, targets, gates, router_t, gate, up, down
):
    steps = nz // 2
    rows, width = normed.shape
    half_width = gate.shape[1]
    lines = -(-(width // LANES + 1) // 16) * 16
    vmem = pl.BlockSpec(memory_space=pltpu.VMEM)
    anywhere = pl.BlockSpec(memory_space=pl.ANY)
    dma = pltpu.SemaphoreType.DMA
    scratch = [
        pltpu.VMEM((width, half_width), BF16),
        pltpu.VMEM((width, half_width), BF16),
        pltpu.VMEM((half_width, width), BF16),
        pltpu.VMEM((steps, 4, 2 * cap, width), BF16),
        pltpu.VMEM((steps, 2 * cap, width), F32),
        pltpu.VMEM((steps, 2 * cap, width), BF16),
        pltpu.VMEM((steps, 2 * cap, width), BF16),
        pltpu.VMEM((steps, 2, 8, LANES), F32),
        pltpu.VMEM((steps, 2, 8, LANES), F32),
        pltpu.VMEM((steps, 2, 8, LANES), F32),
        pltpu.VMEM((steps, 2, 2 * cap, width // 2), BF16),
        pltpu.VMEM((nz, 2 * cap, width // 2), BF16),
        pltpu.VMEM((steps, 2, 8, LANES), F32),
        pltpu.VMEM((nz, 8, LANES), F32),
        pltpu.VMEM((2, 2 * rows, nz * 2 * cap), BF16),
        pltpu.VMEM((nz, lines, LANES), F32),
        pltpu.VMEM((nz, lines, LANES), BF16),
        pltpu.VMEM((nz, lines, LANES), BF16),
        pltpu.VMEM((lines, LANES), F32),
        pltpu.VMEM((lines, LANES), F32),
        pltpu.VMEM((lines, LANES), BF16),
        pltpu.VMEM((nz, lines, LANES), BF16),
        dma((3,)),
        dma((5,)),
        dma((steps, 2)),
        dma((steps, 2)),
        dma((steps, 2)),
        dma((steps, 2)),
        dma((steps,)),
        dma((steps,)),
        dma((steps,)),
        dma((steps,)),
        dma((steps, 2)),
        dma((steps, 2)),
        dma((steps, 2)),
        dma((steps, 2)),
        dma((nz,)),
        dma((nz,)),
        dma((1,)),
        dma((1,)),
        dma((nz,)),
        dma((nz,)),
    ]
    return pl.pallas_call(
        functools.partial(kernel, nz, cap),
        out_shape=(
            jax.ShapeDtypeStruct((rows, width), BF16),
            jax.ShapeDtypeStruct((nz, lines, LANES), F32),
        ),
        in_specs=[vmem] * 10 + [anywhere] * 3,
        out_specs=(vmem, vmem),
        scratch_shapes=scratch,
        compiler_params=pltpu.CompilerParams(
            collective_id=0, has_side_effects=True, vmem_limit_bytes=52 * 1024 * 1024
        ),
        cost_estimate=pl.CostEstimate(
            flops=8_000_000_000, bytes_accessed=8_000_000, transcendentals=200_000
        ),
    )(disp, normed, arriving, returned, inv, gain, picks, targets, gates, router_t, gate, up, down)


def per_device(
    activations,
    cotangents,
    norm_gain,
    routes,
    lengths,
    router_weight,
    gate_weight,
    up_weight,
    down_weight,
):
    arriving = from_behind(activations, "section", 1)[0]
    returned = from_behind(cotangents, "section", -1)[0]
    rows, width = arriving.shape
    experts = router_weight.shape[2]
    top = routes.shape[2]
    cap = 3 * rows * top // (2 * experts)
    picks = routes[0]
    expert_ids = jnp.arange(experts, dtype=jnp.int32)
    onehot = picks[:, :, None] == expert_ids[None, None, :]
    live = (jnp.arange(rows, dtype=jnp.int32) < lengths[0, 0])[:, None]
    hot = (jnp.any(onehot, axis=1) & live).astype(BF16)
    order = jnp.arange(rows, dtype=jnp.int32)
    earlier = (order[:, None] > order[None, :]).astype(BF16)
    before = dot(earlier, hot)
    place = jnp.sum(jnp.where(onehot, before[:, None, :], 0.0), axis=2).astype(jnp.int32)
    targets = jnp.where(live, picks * (2 * cap) + place, -4 * cap)
    slots = jnp.arange(experts * 2 * cap, dtype=jnp.int32)
    select_x = jnp.any(targets[:, :, None] == slots[None, None, :], axis=1)
    select_g = jnp.any(targets[:, :, None] + cap == slots[None, None, :], axis=1)
    full = arriving.astype(F32)
    inv = lax.rsqrt(jnp.mean(full * full, axis=-1, keepdims=True) + EPSILON)
    normed = (full * inv * norm_gain[0].astype(F32)).astype(BF16)
    disp = dot(
        jnp.concatenate([select_x, select_g], axis=0).astype(BF16),
        jnp.concatenate([normed, returned], axis=0),
        (0, 0),
    ).astype(BF16)
    disp = disp.reshape(experts, 2 * cap, width)
    logits = jnp.dot(normed, router_weight[0], preferred_element_type=F32)
    chosen = jnp.sum(jnp.where(onehot, logits[:, None, :], 0.0), axis=2)
    gates = 1.0 / jnp.sum(jnp.exp(chosen[:, None, :] - chosen[:, :, None]), axis=2)
    lig, totals = exchange(
        experts,
        cap,
        disp,
        normed,
        arriving,
        returned,
        inv,
        norm_gain,
        picks,
        targets,
        gates,
        router_weight[0].T,
        gate_weight[0, 0],
        up_weight[0, 0],
        down_weight[0, 0],
    )
    blocks = width // LANES
    router_grad = totals[:, :blocks, :].reshape(experts, width).T
    gain_grad = totals[:, blocks, :].reshape(width)
    return (lig[None], router_grad[None], gain_grad[None])


def solution(mesh):
    in_specs = (
        P("section", "expert", None),
        P("section", "expert", None),
        P("section", None),
        P("section", "expert", None),
        P("section", "expert"),
        P("section", None, None),
        P("section", "expert", None, None),
        P("section", "expert", None, None),
        P("section", "expert", None, None),
    )
    out_specs = (P("section", "expert", None), P("section", None, None), P("section", None))
    return jax.shard_map(
        per_device, mesh=mesh, in_specs=in_specs, out_specs=out_specs, check_vma=False
    )
```

```python
import functools
import types

import jax
import jax.numpy as jnp
from jax import lax
from jax.experimental import pallas as pl
from jax.experimental.pallas import tpu as pltpu
from jax.sharding import PartitionSpec as P

EPSILON = 1e-05
LANES = 128
G_PIECES = 4
X_PIECES = 1
MESH = pl.DeviceIdType.MESH
F32 = jnp.float32
BF16 = jnp.bfloat16


def dot(a, b, contract=(1, 0)):
    return lax.dot_general(
        a, b, (((contract[0],), (contract[1],)), ((), ())), preferred_element_type=F32
    )


def split(value):
    high = value.astype(BF16)
    return high, (value - high.astype(F32)).astype(BF16)


def iota(shape, dim):
    return lax.broadcasted_iota(jnp.int32, shape, dim)


def kernel(nz, cap, sections, names, *refs):
    r = types.SimpleNamespace(**dict(zip(names, refs)))
    steps = nz // 2
    width, half_width = r.gate_w.shape
    half_model = width // 2
    rows = r.normed.shape[0]
    g_wide = half_model // G_PIECES
    x_wide = half_model // X_PIECES
    blocks = width // LANES
    section = lax.axis_index("section")
    me = lax.axis_index("expert")
    chip = me // 2
    core = me - chip * 2
    sibling = chip * 2 + 1 - core
    section_before = lax.rem(section + sections - 1, sections)
    section_after = lax.rem(section + 1, sections)

    def at_offset(offset):
        return lax.rem(chip + offset + nz, nz) * 2 + core

    def remote(src, dst, sems, index, target, home=section):
        return pltpu.make_async_remote_copy(
            src_ref=src,
            dst_ref=dst,
            send_sem=sems[0].at[index],
            recv_sem=sems[1].at[index],
            device_id=(home, target),
            device_id_type=MESH,
        )

    def offset_of(step, side):
        return steps - step if side == 0 else lax.rem(steps + step, nz)

    def hand_on(part, piece):
        columns = pl.ds((2 * piece + part) * x_wide, x_wide)
        return remote(
            r.acts.at[0, :, columns],
            r.xex.at[piece, pl.ds(part * rows, rows), :],
            (r.xe_send, r.xe_recv),
            2 * piece + part,
            me,
            section_after,
        )

    def hand_back(part, piece):
        columns = pl.ds((2 * piece + part) * g_wide, g_wide)
        return remote(
            r.cots.at[0, :, columns],
            r.gex.at[piece, pl.ds(part * rows, rows), :],
            (r.ge_send, r.ge_recv),
            2 * piece + part,
            me,
            section_before,
        )

    def dispatch_g(piece, step, side):
        target = at_offset(offset_of(step, side))
        return remote(
            r.dispg.at[piece, target // 2],
            r.gbuf.at[step, side, piece],
            (r.gd_send, r.gd_recv),
            (piece, step, side),
            target,
        )

    def dispatch_x(piece, step, side):
        target = at_offset(offset_of(step, side))
        return remote(
            r.dispx.at[piece, target // 2],
            r.xbuf.at[step, side, piece],
            (r.xd_send, r.xd_recv),
            (piece, step, side),
            target,
        )

    def forward_g(step, side):
        return remote(
            r.gbuf.at[step, side],
            r.gbuf.at[step, 2 + side],
            (r.gf_send, r.gf_recv),
            (step, side),
            sibling,
        )

    def forward_x(step, side):
        return remote(
            r.xbuf.at[step, side],
            r.xbuf.at[step, 2 + side],
            (r.xf_send, r.xf_recv),
            (step, side),
            sibling,
        )

    def partial(step):
        return remote(r.psend.at[step], r.precv.at[step], (r.p_send, r.p_recv), step, sibling)

    def partial_share(step):
        return remote(
            r.share_send.at[step], r.share_recv.at[step], (r.h_send, r.h_recv), step, sibling
        )

    def give_back(step, side):
        target = at_offset(-offset_of(step, side))
        return remote(
            r.rsend.at[step, side], r.ret.at[chip], (r.r_send, r.r_recv), (step, side), target
        )

    def give_share(step, side):
        target = at_offset(-offset_of(step, side))
        return remote(
            r.ssend.at[step, side], r.sret.at[chip], (r.s_send, r.s_recv), (step, side), target
        )

    def reduce_router(offset):
        target = at_offset(offset)
        return remote(
            r.q_src.at[target // 2], r.q_dst.at[offset], (r.q_send, r.q_recv), offset, target
        )

    def gather_router(offset):
        return remote(
            r.a_src, r.a_dst.at[chip], (r.a_send, r.a_recv), offset, at_offset(offset)
        )

    def gather_gain(offset):
        return remote(
            r.n_src, r.n_dst.at[offset], (r.n_send, r.n_recv), offset, at_offset(offset)
        )

    def pairs(body):
        def both(step, carry):
            body(step, 0)

            @pl.when(step > 0)
            def _():
                body(step, 1)

            return carry

        lax.fori_loop(0, steps, both, 0)

    def others(body):
        def one(offset, carry):
            body(offset)
            return carry

        lax.fori_loop(1, nz, one, 0)

    loads = [
        pltpu.make_async_copy(r.gate_hbm, r.gate_w, r.w_sem.at[0]),
        pltpu.make_async_copy(r.up_hbm, r.up_w, r.w_sem.at[1]),
        pltpu.make_async_copy(r.down_hbm, r.down_w, r.w_sem.at[2]),
    ]
    for load in loads:
        load.start()

    live = iota((1, rows), 1) < r.lengths[...]
    named = [iota((nz, rows), 0) == r.picks[k : k + 1, :] for k in range(2)]
    hot = jnp.where((named[0] | named[1]) & live, 1.0, 0.0).astype(BF16)
    earlier = jnp.where(iota((rows, rows), 0) < iota((rows, rows), 1), 1.0, 0.0).astype(BF16)
    before = dot(hot, earlier)
    targets = []
    for k in range(2):
        place = jnp.sum(jnp.where(named[k], before, 0.0), axis=0, keepdims=True)
        slot = r.picks[k : k + 1, :] * (2 * cap) + place.astype(jnp.int32)
        targets.append(jnp.where(live, slot, -4 * cap))
    slots = iota((nz * 2 * cap, rows), 0)
    for part in range(2):
        chosen = (slots == targets[0] + part * cap) | (slots == targets[1] + part * cap)
        r.select[:, part * rows : (part + 1) * rows] = jnp.where(chosen, 1.0, 0.0).astype(BF16)

    barrier = pltpu.get_barrier_semaphore()

    def greet(offset):
        pl.semaphore_signal(
            barrier, inc=1, device_id=(section, at_offset(offset)), device_id_type=MESH
        )

    others(greet)
    for home, target in ((section, sibling), (section_before, me), (section_after, me)):
        pl.semaphore_signal(barrier, inc=1, device_id=(home, target), device_id_type=MESH)
    pl.semaphore_wait(barrier, nz + 2)

    for piece in range(G_PIECES):
        for part in range(2):
            hand_back(part, piece).start()
    for piece in range(X_PIECES):
        for part in range(2):
            hand_on(part, piece).start()

    own_copies = []
    for piece in range(G_PIECES):
        for part in range(2):
            hand_back(part, piece).wait_recv()
        spread = dot(r.select[...], r.gex[piece]).astype(BF16)
        r.dispg[piece] = spread.reshape(nz, 2 * cap, g_wide)
        pairs(lambda step, side, piece=piece: dispatch_g(piece, step, side).start())
        own_copies.append(
            pltpu.make_async_copy(
                r.dispg.at[piece, chip], r.gbuf.at[0, 1, piece], r.l_sem.at[len(own_copies)]
            )
        )
        own_copies[-1].start()

    for piece in range(X_PIECES):
        for part in range(2):
            hand_on(part, piece).wait_recv()

    def sides(ref, count):
        parts = [
            ref[piece, part * rows : (part + 1) * rows, :]
            for piece in range(count)
            for part in range(2)
        ]
        return jnp.concatenate(parts, axis=1)

    full = sides(r.xex, X_PIECES).astype(F32)
    inv = lax.rsqrt(jnp.mean(full * full, axis=-1, keepdims=True) + EPSILON)
    r.normed[...] = (full * inv * r.gain[...].astype(F32)).astype(BF16)
    for piece in range(X_PIECES):
        start = 2 * piece * x_wide
        both = jnp.concatenate(
            [r.normed[:, start : start + x_wide], r.normed[:, start + x_wide : start + 2 * x_wide]],
            axis=0,
        )
        spread = dot(r.select[...], both).astype(BF16)
        r.dispx[piece] = spread.reshape(nz, 2 * cap, x_wide)
        pairs(lambda step, side, piece=piece: dispatch_x(piece, step, side).start())
        own_copies.append(
            pltpu.make_async_copy(
                r.dispx.at[piece, chip], r.xbuf.at[0, 1, piece], r.l_sem.at[len(own_copies)]
            )
        )
        own_copies[-1].start()

    same = iota((rows, rows), 0) == iota((rows, rows), 1)

    def upright(line):
        return jnp.sum(jnp.where(same, line, 0), axis=1, keepdims=True)

    expert_ids = iota((rows, nz), 1)
    picked = [upright(r.picks[k : k + 1, :]) for k in range(2)]
    target_of = [upright(targets[k]) for k in range(2)]
    logits = dot(r.normed[...], r.router_t[...], (1, 1))
    scores = [
        jnp.sum(jnp.where(expert_ids == picked[k], logits, 0.0), axis=1, keepdims=True)
        for k in range(2)
    ]
    gates = [1.0 / (1.0 + jnp.exp(scores[1 - k] - scores[k])) for k in range(2)]
    across_slots = iota((rows, nz * 2 * cap), 1)
    for part in range(2):
        mix = jnp.where(across_slots == target_of[0] + part * cap, gates[0], 0.0)
        mix = mix + jnp.where(across_slots == target_of[1] + part * cap, gates[1], 0.0)
        r.weights[part * rows : (part + 1) * rows, :] = mix.astype(BF16)

    for copy in own_copies:
        copy.wait()
    for load in loads:
        load.wait()

    def pick_rows(value, part):
        return value.reshape(4, 2 * cap, half_width)[:, part * cap : (part + 1) * cap].reshape(
            4 * cap, half_width
        )

    def receive_g(step):
        for piece in range(G_PIECES):
            dispatch_g(piece, step, 0).wait_recv()
        forward_g(step, 0).start()

        @pl.when(step > 0)
        def _():
            for piece in range(G_PIECES):
                dispatch_g(piece, step, 1).wait_recv()

        forward_g(step, 1).start()

    def compute_g(step):
        for side in range(2):
            forward_g(step, side).wait_recv()
        total = jnp.zeros((4 * cap, half_width), F32)
        for piece in range(G_PIECES):
            block = r.gbuf[step, :, piece].reshape(8 * cap, g_wide)
            for part in range(2):
                start = (2 * piece + part) * g_wide
                down = r.down_w[:, start : start + g_wide]
                total = total + pick_rows(dot(block, down, (1, 1)), part)
        r.hidden_grad[step] = total

    def receive_x(step):
        for piece in range(X_PIECES):
            dispatch_x(piece, step, 0).wait_recv()
        forward_x(step, 0).start()

        @pl.when(step > 0)
        def _():
            for piece in range(X_PIECES):
                dispatch_x(piece, step, 1).wait_recv()

        forward_x(step, 1).start()

    diagonal = iota((cap, LANES), 0) == iota((cap, LANES), 1)

    def compute_x(step):
        for side in range(2):
            forward_x(step, side).wait_recv()
        gate_pre = jnp.zeros((4 * cap, half_width), F32)
        up_pre = jnp.zeros((4 * cap, half_width), F32)
        for piece in range(X_PIECES):
            block = r.xbuf[step, :, piece].reshape(8 * cap, x_wide)
            for part in range(2):
                start = (2 * piece + part) * x_wide
                columns = slice(start, start + x_wide)
                gate_pre = gate_pre + pick_rows(dot(block, r.gate_w[columns, :]), part)
                up_pre = up_pre + pick_rows(dot(block, r.up_w[columns, :]), part)
        hidden_grad = r.hidden_grad[step]
        logistic = jax.nn.sigmoid(gate_pre)
        activated = gate_pre * logistic
        share = jnp.sum(activated * up_pre * hidden_grad, axis=1, keepdims=True)
        for which in range(4):
            column = share[which * cap : (which + 1) * cap]
            line = jnp.sum(jnp.where(diagonal, column, 0.0), axis=0, keepdims=True)
            tile = jnp.broadcast_to(line, (8, LANES))
            if which < 2:
                r.own_share[step, which] = tile
            else:
                r.share_send[step, which - 2] = tile
        partial_share(step).start()
        gate_grad = (
            hidden_grad * up_pre * logistic * (1.0 + gate_pre * (1.0 - logistic))
        ).astype(BF16)
        up_grad = (hidden_grad * activated).astype(BF16)
        chunk = min(512, width)
        for start in range(0, width, chunk):
            columns = slice(start, start + chunk)
            back = dot(gate_grad, r.gate_w[columns, :], (1, 1)) + dot(
                up_grad, r.up_w[columns, :], (1, 1)
            )
            r.own[step, :, columns] = back[: 2 * cap]
            r.psend[step, :, columns] = back[2 * cap :].astype(BF16)
        partial(step).start()

    def finish(step):
        partial_share(step).wait_recv()
        for side in range(2):
            r.ssend[step, side] = r.own_share[step, side] + r.share_recv[step, side]
        give_share(step, 0).start()

        @pl.when(step > 0)
        def _():
            give_share(step, 1).start()

        partial(step).wait_recv()
        total = r.own[step] + r.precv[step].astype(F32)
        for side in range(2):
            mine = total[side * cap : (side + 1) * cap]
            stacked = jnp.concatenate([mine[:, :half_model], mine[:, half_model:]], axis=0)
            r.rsend[step, side] = stacked.astype(BF16)
        give_back(step, 0).start()

        @pl.when(step > 0)
        def _():
            give_back(step, 1).start()

    def pipeline_g(turn, carry):
        @pl.when(turn < steps)
        def _():
            receive_g(turn)

        @pl.when(turn >= 1)
        def _():
            compute_g(turn - 1)

        return carry

    def pipeline_x(turn, carry):
        @pl.when(turn < steps)
        def _():
            receive_x(turn)

        @pl.when((turn >= 1) & (turn <= steps))
        def _():
            compute_x(turn - 1)

        @pl.when(turn >= 2)
        def _():
            finish(turn - 2)

        return carry

    lax.fori_loop(0, steps + 1, pipeline_g, 0)
    lax.fori_loop(0, steps + 2, pipeline_x, 0)

    base = G_PIECES + X_PIECES
    self_back = pltpu.make_async_copy(r.rsend.at[0, 1], r.ret.at[chip], r.l_sem.at[base])
    self_share = pltpu.make_async_copy(r.ssend.at[0, 1], r.sret.at[chip], r.l_sem.at[base + 1])
    self_back.start()
    self_share.start()
    self_share.wait()
    pairs(lambda step, side: give_share(step, side).wait_recv())

    shares = jnp.max(r.sret[...], axis=1)
    places = iota((rows, LANES), 1)
    first, second = split(shares)
    third = (shares - first.astype(F32) - second.astype(F32)).astype(BF16)
    gate_share = []
    for k in range(2):
        onehot = jnp.where(expert_ids == picked[k], 1.0, 0.0).astype(BF16)
        line = dot(onehot, first) + dot(onehot, second) + dot(onehot, third)
        place = target_of[k] - picked[k] * (2 * cap)
        gate_share.append(jnp.sum(jnp.where(places == place, line, 0.0), axis=1, keepdims=True))
    mean_share = gates[0] * gate_share[0] + gates[1] * gate_share[1]
    logit_grad = jnp.zeros((rows, nz), F32)
    for k in range(2):
        select_grad = gates[k] * (gate_share[k] - mean_share)
        logit_grad = logit_grad + jnp.where(expert_ids == picked[k], select_grad, 0.0)
    grad_high, grad_low = split(logit_grad)
    router_term = dot(grad_high, r.normed[...], (0, 0)) + dot(grad_low, r.normed[...], (0, 0))
    for block in range(blocks):
        r.stage[:, block, :] = router_term[:, block * LANES : (block + 1) * LANES]
    r.q_src[...] = r.stage[...].astype(BF16)
    others(lambda offset: reduce_router(offset).start())
    self_reduce = pltpu.make_async_copy(r.q_src.at[chip], r.q_dst.at[0], r.l_sem.at[base + 2])
    self_reduce.start()
    router_part = dot(grad_high, r.router_t[...]) + dot(grad_low, r.router_t[...])

    self_back.wait()
    pairs(lambda step, side: give_back(step, side).wait_recv())
    came_back = r.ret[...].reshape(nz * 2 * cap, half_model)
    both = dot(r.weights[...], came_back)
    normed_grad = jnp.concatenate([both[:rows], both[rows:]], axis=1) + router_part
    unit = sides(r.xex, X_PIECES).astype(F32) * inv
    gain_term = jnp.sum(normed_grad * unit, axis=0, keepdims=True)
    for block in range(blocks):
        r.gain_stage[block : block + 1, :] = gain_term[:, block * LANES : (block + 1) * LANES]
    r.n_src[...] = r.gain_stage[...].astype(BF16)
    others(lambda offset: gather_gain(offset).start())
    r.n_dst[0] = r.n_src[...]

    self_reduce.wait()
    others(lambda offset: reduce_router(offset).wait_recv())
    r.x_src[...] = jnp.sum(r.q_dst[...].astype(F32), axis=0)
    across_router = remote(r.x_src, r.x_dst, (r.x_send, r.x_recv), 0, sibling)
    across_router.start()

    scaled = normed_grad * r.gain[...].astype(F32)
    mean_scaled = jnp.mean(scaled * unit, axis=-1, keepdims=True)
    returned = sides(r.gex, G_PIECES).astype(F32)
    r.lig[...] = (returned + inv * (scaled - unit * mean_scaled)).astype(BF16)

    across_router.wait_recv()
    r.a_src[...] = (r.x_src[...] + r.x_dst[...]).astype(BF16)
    others(lambda offset: gather_router(offset).start())
    r.a_dst[chip] = r.a_src[...]

    others(lambda offset: gather_gain(offset).wait_recv())
    r.y_src[...] = jnp.sum(r.n_dst[...].astype(F32), axis=0)
    across_gain = remote(r.y_src, r.y_dst, (r.x_send, r.x_recv), 1, sibling)
    across_gain.start()

    for piece in range(G_PIECES):
        for part in range(2):
            hand_back(part, piece).wait_send()
        pairs(lambda step, side, piece=piece: dispatch_g(piece, step, side).wait_send())
    for piece in range(X_PIECES):
        for part in range(2):
            hand_on(part, piece).wait_send()
        pairs(lambda step, side, piece=piece: dispatch_x(piece, step, side).wait_send())

    def drain(step, carry):
        for side in range(2):
            forward_g(step, side).wait_send()
            forward_x(step, side).wait_send()
        partial(step).wait_send()
        partial_share(step).wait_send()
        return carry

    lax.fori_loop(0, steps, drain, 0)
    pairs(lambda step, side: give_back(step, side).wait_send())
    pairs(lambda step, side: give_share(step, side).wait_send())
    others(lambda offset: reduce_router(offset).wait_send())
    others(lambda offset: gather_gain(offset).wait_send())

    across_router.wait_send()
    across_gain.wait()
    r.gain_total[...] = r.y_src[...] + r.y_dst[...]
    others(lambda offset: gather_router(offset).wait())
    for block in range(blocks):
        r.router_total[:, block * LANES : (block + 1) * LANES] = r.a_dst[:, block, :].astype(F32)


def exchange(nz, cap, sections, lengths, picks, gain, router_t, acts, cots, gate, up, down):
    steps = nz // 2
    rows, width = acts.shape[1:]
    half_width = gate.shape[1]
    half_model = width // 2
    lines = width // LANES
    g_wide = half_model // G_PIECES
    x_wide = half_model // X_PIECES
    vmem = pl.BlockSpec(memory_space=pltpu.VMEM)
    anywhere = pl.BlockSpec(memory_space=pl.ANY)

    def sems(*shape):
        return pltpu.SemaphoreType.DMA(shape)

    tall = -(-lines // 16) * 16
    scratch = {
        "gate_w": pltpu.VMEM((width, half_width), BF16),
        "up_w": pltpu.VMEM((width, half_width), BF16),
        "down_w": pltpu.VMEM((half_width, width), BF16),
        "select": pltpu.VMEM((nz * 2 * cap, 2 * rows), BF16),
        "gex": pltpu.VMEM((G_PIECES, 2 * rows, g_wide), BF16),
        "xex": pltpu.VMEM((X_PIECES, 2 * rows, x_wide), BF16),
        "normed": pltpu.VMEM((rows, width), BF16),
        "dispg": pltpu.VMEM((G_PIECES, nz, 2 * cap, g_wide), BF16),
        "dispx": pltpu.VMEM((X_PIECES, nz, 2 * cap, x_wide), BF16),
        "gbuf": pltpu.VMEM((steps, 4, G_PIECES, 2 * cap, g_wide), BF16),
        "xbuf": pltpu.VMEM((steps, 4, X_PIECES, 2 * cap, x_wide), BF16),
        "hidden_grad": pltpu.VMEM((steps, 4 * cap, half_width), F32),
        "own": pltpu.VMEM((steps, 2 * cap, width), F32),
        "psend": pltpu.VMEM((steps, 2 * cap, width), BF16),
        "precv": pltpu.VMEM((steps, 2 * cap, width), BF16),
        "own_share": pltpu.VMEM((steps, 2, 8, LANES), F32),
        "share_send": pltpu.VMEM((steps, 2, 8, LANES), F32),
        "share_recv": pltpu.VMEM((steps, 2, 8, LANES), F32),
        "rsend": pltpu.VMEM((steps, 2, 2 * cap, half_model), BF16),
        "ret": pltpu.VMEM((nz, 2 * cap, half_model), BF16),
        "ssend": pltpu.VMEM((steps, 2, 8, LANES), F32),
        "sret": pltpu.VMEM((nz, 8, LANES), F32),
        "weights": pltpu.VMEM((2 * rows, nz * 2 * cap), BF16),
        "stage": pltpu.VMEM((nz, tall, LANES), F32),
        "gain_stage": pltpu.VMEM((tall, LANES), F32),
        "q_src": pltpu.VMEM((nz, tall, LANES), BF16),
        "q_dst": pltpu.VMEM((nz, tall, LANES), BF16),
        "x_src": pltpu.VMEM((tall, LANES), F32),
        "x_dst": pltpu.VMEM((tall, LANES), F32),
        "y_src": pltpu.VMEM((tall, LANES), F32),
        "y_dst": pltpu.VMEM((tall, LANES), F32),
        "a_src": pltpu.VMEM((tall, LANES), BF16),
        "a_dst": pltpu.VMEM((nz, tall, LANES), BF16),
        "n_src": pltpu.VMEM((tall, LANES), BF16),
        "n_dst": pltpu.VMEM((nz, tall, LANES), BF16),
        "w_sem": sems(3),
        "l_sem": sems(G_PIECES + X_PIECES + 3),
        "ge_send": sems(2 * G_PIECES),
        "ge_recv": sems(2 * G_PIECES),
        "xe_send": sems(2 * X_PIECES),
        "xe_recv": sems(2 * X_PIECES),
        "gd_send": sems(G_PIECES, steps, 2),
        "gd_recv": sems(G_PIECES, steps, 2),
        "xd_send": sems(X_PIECES, steps, 2),
        "xd_recv": sems(X_PIECES, steps, 2),
        "gf_send": sems(steps, 2),
        "gf_recv": sems(steps, 2),
        "xf_send": sems(steps, 2),
        "xf_recv": sems(steps, 2),
        "p_send": sems(steps),
        "p_recv": sems(steps),
        "h_send": sems(steps),
        "h_recv": sems(steps),
        "r_send": sems(steps, 2),
        "r_recv": sems(steps, 2),
        "s_send": sems(steps, 2),
        "s_recv": sems(steps, 2),
        "q_send": sems(nz),
        "q_recv": sems(nz),
        "x_send": sems(2),
        "x_recv": sems(2),
        "a_send": sems(nz),
        "a_recv": sems(nz),
        "n_send": sems(nz),
        "n_recv": sems(nz),
    }
    operands = ["lengths", "picks", "gain", "router_t", "acts", "cots"]
    operands += ["gate_hbm", "up_hbm", "down_hbm"]
    names = operands + ["lig", "router_total", "gain_total"] + list(scratch)
    return pl.pallas_call(
        functools.partial(kernel, nz, cap, sections, names),
        out_shape=(
            jax.ShapeDtypeStruct((rows, width), BF16),
            jax.ShapeDtypeStruct((nz, width), F32),
            jax.ShapeDtypeStruct((tall, LANES), F32),
        ),
        in_specs=[vmem] * 4 + [anywhere] * 5,
        out_specs=(vmem, vmem, vmem),
        scratch_shapes=list(scratch.values()),
        compiler_params=pltpu.CompilerParams(
            collective_id=0, has_side_effects=True, vmem_limit_bytes=56 * 1024 * 1024
        ),
        cost_estimate=pl.CostEstimate(
            flops=8_000_000_000, bytes_accessed=8_000_000, transcendentals=200_000
        ),
    )(lengths, picks, gain, router_t, acts, cots, gate, up, down)


def per_device(
    activations,
    cotangents,
    norm_gain,
    routes,
    lengths,
    router_weight,
    gate_weight,
    up_weight,
    down_weight,
):
    rows, width = activations.shape[1:]
    experts = router_weight.shape[2]
    top = routes.shape[2]
    cap = 3 * rows * top // (2 * experts)
    lig, router_total, gain_total = exchange(
        experts,
        cap,
        lax.axis_size("section"),
        lengths,
        routes[0].T,
        norm_gain,
        router_weight[0].T,
        activations,
        cotangents,
        gate_weight[0, 0],
        up_weight[0, 0],
        down_weight[0, 0],
    )
    lines = width // LANES
    return (lig[None], router_total.T[None], gain_total[:lines].reshape(1, width))


def solution(mesh):
    in_specs = (
        P("section", "expert", None),
        P("section", "expert", None),
        P("section", None),
        P("section", "expert", None),
        P("section", "expert"),
        P("section", None, None),
        P("section", "expert", None, None),
        P("section", "expert", None, None),
        P("section", "expert", None, None),
    )
    out_specs = (P("section", "expert", None), P("section", None, None), P("section", None))
    return jax.shard_map(
        per_device, mesh=mesh, in_specs=in_specs, out_specs=out_specs, check_vma=False
    )
```

```python
import functools
import types

import jax
import jax.numpy as jnp
from jax import lax
from jax.experimental import pallas as pl
from jax.experimental.pallas import tpu as pltpu
from jax.sharding import PartitionSpec as P

EPSILON = 1e-05
LANES = 128
G_PIECES = 4
X_PIECES = 1
MESH = pl.DeviceIdType.MESH
F32 = jnp.float32
BF16 = jnp.bfloat16


def dot(a, b, contract=(1, 0)):
    return lax.dot_general(
        a, b, (((contract[0],), (contract[1],)), ((), ())), preferred_element_type=F32
    )


def split(value):
    high = value.astype(BF16)
    return high, (value - high.astype(F32)).astype(BF16)


def iota(shape, dim):
    return lax.broadcasted_iota(jnp.int32, shape, dim)


def kernel(nz, cap, sections, names, *refs):
    r = types.SimpleNamespace(**dict(zip(names, refs)))
    steps = nz // 2
    width, half_width = r.gate_w.shape
    half_model = width // 2
    rows = r.normed.shape[0]
    g_wide = half_model // G_PIECES
    x_wide = half_model // X_PIECES
    blocks = width // LANES
    r_first, r_second = steps // 2, 3 * steps // 4
    section = lax.axis_index("section")
    me = lax.axis_index("expert")
    chip = me // 2
    core = me - chip * 2
    sibling = chip * 2 + 1 - core
    section_before = lax.rem(section + sections - 1, sections)
    section_after = lax.rem(section + 1, sections)

    def at_offset(offset):
        return lax.rem(chip + offset + nz, nz) * 2 + core

    def remote(src, dst, sems, index, target, home=section):
        return pltpu.make_async_remote_copy(
            src_ref=src,
            dst_ref=dst,
            send_sem=sems[0].at[index],
            recv_sem=sems[1].at[index],
            device_id=(home, target),
            device_id_type=MESH,
        )

    def offset_of(step, side):
        return steps - step if side == 0 else lax.rem(steps + step, nz)

    def hand_on(part, piece):
        columns = pl.ds((2 * piece + part) * x_wide, x_wide)
        return remote(
            r.acts.at[0, :, columns],
            r.xex.at[piece, pl.ds(part * rows, rows), :],
            (r.xe_send, r.xe_recv),
            2 * piece + part,
            me,
            section_after,
        )

    def hand_back(part, piece):
        columns = pl.ds((2 * piece + part) * g_wide, g_wide)
        return remote(
            r.cots.at[0, :, columns],
            r.gex.at[piece, pl.ds(part * rows, rows), :],
            (r.ge_send, r.ge_recv),
            2 * piece + part,
            me,
            section_before,
        )

    def dispatch_g(piece, step, side):
        target = at_offset(offset_of(step, side))
        return remote(
            r.dispg.at[piece, target // 2],
            r.gbuf.at[step, side, piece],
            (r.gd_send, r.gd_recv),
            (piece, step, side),
            target,
        )

    def dispatch_x(piece, step, side):
        target = at_offset(offset_of(step, side))
        return remote(
            r.dispx.at[piece, target // 2],
            r.xbuf.at[step, side, piece],
            (r.xd_send, r.xd_recv),
            (piece, step, side),
            target,
        )

    def forward_g(step, side):
        return remote(
            r.gbuf.at[step, side],
            r.gbuf.at[step, 2 + side],
            (r.gf_send, r.gf_recv),
            (step, side),
            sibling,
        )

    def forward_x(step, side):
        return remote(
            r.xbuf.at[step, side],
            r.xbuf.at[step, 2 + side],
            (r.xf_send, r.xf_recv),
            (step, side),
            sibling,
        )

    def partial(step):
        return remote(r.psend.at[step], r.precv.at[step], (r.p_send, r.p_recv), step, sibling)

    def partial_share(step):
        return remote(
            r.share_send.at[step], r.share_recv.at[step], (r.h_send, r.h_recv), step, sibling
        )

    def give_back(step, side):
        target = at_offset(-offset_of(step, side))
        return remote(
            r.rsend.at[step, side], r.ret.at[chip], (r.r_send, r.r_recv), (step, side), target
        )

    def give_share(step, side):
        target = at_offset(-offset_of(step, side))
        return remote(
            r.ssend.at[step, side], r.sret.at[chip], (r.s_send, r.s_recv), (step, side), target
        )

    def give_gates(step, side):
        target = at_offset(offset_of(step, side))
        return remote(
            r.gate_out.at[target // 2],
            r.gate_in.at[step, side],
            (r.gg_send, r.gg_recv),
            (step, side),
            target,
        )

    def reduce_router(offset):
        target = at_offset(offset)
        return remote(
            r.q_src.at[target // 2], r.q_dst.at[offset], (r.q_send, r.q_recv), offset, target
        )

    def gather_router(offset):
        return remote(
            r.a_src, r.a_dst.at[chip], (r.a_send, r.a_recv), offset, at_offset(offset)
        )

    def pairs(body, first=0, last=steps):
        def both(step, carry):
            body(step, 0)

            @pl.when(step > 0)
            def _():
                body(step, 1)

            return carry

        lax.fori_loop(first, last, both, 0)

    def others(body):
        def one(offset, carry):
            body(offset)
            return carry

        lax.fori_loop(1, nz, one, 0)

    barrier = pltpu.get_barrier_semaphore()

    def greet(offset):
        pl.semaphore_signal(
            barrier, inc=1, device_id=(section, at_offset(offset)), device_id_type=MESH
        )

    others(greet)
    for home, target in ((section, sibling), (section_before, me), (section_after, me)):
        pl.semaphore_signal(barrier, inc=1, device_id=(home, target), device_id_type=MESH)
    loads = [
        pltpu.make_async_copy(r.gate_hbm, r.gate_w, r.w_sem.at[0]),
        pltpu.make_async_copy(r.up_hbm, r.up_w, r.w_sem.at[1]),
        pltpu.make_async_copy(r.down_hbm, r.down_w, r.w_sem.at[2]),
    ]
    for load in loads:
        load.start()

    live = iota((1, rows), 1) < r.lengths[...]
    named = [iota((nz, rows), 0) == r.picks[k : k + 1, :] for k in range(2)]
    hot = jnp.where((named[0] | named[1]) & live, 1.0, 0.0).astype(BF16)
    earlier = jnp.where(iota((rows, rows), 0) < iota((rows, rows), 1), 1.0, 0.0).astype(BF16)
    before = dot(hot, earlier)
    targets = []
    for k in range(2):
        place = jnp.sum(jnp.where(named[k], before, 0.0), axis=0, keepdims=True)
        slot = r.picks[k : k + 1, :] * (2 * cap) + place.astype(jnp.int32)
        targets.append(jnp.where(live, slot, -4 * cap))
    slots = iota((nz * 2 * cap, rows), 0)
    for part in range(2):
        chosen = (slots == targets[0] + part * cap) | (slots == targets[1] + part * cap)
        r.select[:, part * rows : (part + 1) * rows] = jnp.where(chosen, 1.0, 0.0).astype(BF16)

    pl.semaphore_wait(barrier, nz + 2)

    for piece in range(G_PIECES):
        for part in range(2):
            hand_back(part, piece).start()
    for piece in range(X_PIECES):
        for part in range(2):
            hand_on(part, piece).start()

    own_copies = []
    for piece in range(G_PIECES):
        for part in range(2):
            hand_back(part, piece).wait_recv()
        spread = dot(r.select[...], r.gex[piece]).astype(BF16)
        r.dispg[piece] = spread.reshape(nz, 2 * cap, g_wide)
        pairs(lambda step, side, piece=piece: dispatch_g(piece, step, side).start())
        own_copies.append(
            pltpu.make_async_copy(
                r.dispg.at[piece, chip], r.gbuf.at[0, 1, piece], r.l_sem.at[len(own_copies)]
            )
        )
        own_copies[-1].start()

    for piece in range(X_PIECES):
        for part in range(2):
            hand_on(part, piece).wait_recv()

    def sides(ref, count):
        parts = [
            ref[piece, part * rows : (part + 1) * rows, :]
            for piece in range(count)
            for part in range(2)
        ]
        return jnp.concatenate(parts, axis=1)

    full = sides(r.xex, X_PIECES).astype(F32)
    inv = lax.rsqrt(jnp.mean(full * full, axis=-1, keepdims=True) + EPSILON)
    r.normed[...] = (full * inv * r.gain[...].astype(F32)).astype(BF16)
    for piece in range(X_PIECES):
        start = 2 * piece * x_wide
        both = jnp.concatenate(
            [r.normed[:, start : start + x_wide], r.normed[:, start + x_wide : start + 2 * x_wide]],
            axis=0,
        )
        spread = dot(r.select[...], both).astype(BF16)
        r.dispx[piece] = spread.reshape(nz, 2 * cap, x_wide)
        pairs(lambda step, side, piece=piece: dispatch_x(piece, step, side).start())
        own_copies.append(
            pltpu.make_async_copy(
                r.dispx.at[piece, chip], r.xbuf.at[0, 1, piece], r.l_sem.at[len(own_copies)]
            )
        )
        own_copies[-1].start()

    same = iota((rows, rows), 0) == iota((rows, rows), 1)

    def upright(line):
        return jnp.sum(jnp.where(same, line, 0), axis=1, keepdims=True)

    expert_ids = iota((rows, nz), 1)
    picked = [upright(r.picks[k : k + 1, :]) for k in range(2)]
    target_of = [upright(targets[k]) for k in range(2)]
    logits = dot(r.normed[...], r.router_t[...], (1, 1))
    scores = [
        jnp.sum(jnp.where(expert_ids == picked[k], logits, 0.0), axis=1, keepdims=True)
        for k in range(2)
    ]
    gates = [1.0 / (1.0 + jnp.exp(scores[1 - k] - scores[k])) for k in range(2)]
    places = iota((rows, LANES), 1)
    place_of = [target_of[k] - picked[k] * (2 * cap) for k in range(2)]
    slot_gates = jnp.zeros((nz, LANES), F32)
    for k in range(2):
        onehot = jnp.where(named[k], 1.0, 0.0).astype(BF16)
        for piece in split(jnp.where(places == place_of[k], gates[k], 0.0)):
            slot_gates = slot_gates + dot(onehot, piece)
    r.gate_out[...] = slot_gates.reshape(nz, 1, LANES)
    pairs(lambda step, side: give_gates(step, side).start())
    r.gate_in[0, 1] = r.gate_out[chip]
    r.gain_sum[...] = jnp.zeros_like(r.gain_sum)
    across_slots = iota((rows, nz * 2 * cap), 1)
    for part in range(2):
        mix = jnp.where(across_slots == target_of[0] + part * cap, gates[0], 0.0)
        mix = mix + jnp.where(across_slots == target_of[1] + part * cap, gates[1], 0.0)
        r.weights[part * rows : (part + 1) * rows, :] = mix.astype(BF16)

    for copy in own_copies:
        copy.wait()
    for load in loads:
        load.wait()

    def pick_rows(value, part):
        return value.reshape(4, 2 * cap, half_width)[:, part * cap : (part + 1) * cap].reshape(
            4 * cap, half_width
        )

    def receive_g(step):
        for piece in range(G_PIECES):
            dispatch_g(piece, step, 0).wait_recv()
        forward_g(step, 0).start()

        @pl.when(step > 0)
        def _():
            for piece in range(G_PIECES):
                dispatch_g(piece, step, 1).wait_recv()

        forward_g(step, 1).start()

    def compute_g(step):
        for side in range(2):
            forward_g(step, side).wait_recv()
        total = jnp.zeros((4 * cap, half_width), F32)
        for piece in range(G_PIECES):
            block = r.gbuf[step, :, piece].reshape(8 * cap, g_wide)
            for part in range(2):
                start = (2 * piece + part) * g_wide
                down = r.down_w[:, start : start + g_wide]
                total = total + pick_rows(dot(block, down, (1, 1)), part)
        r.hidden_grad[step] = total

    def receive_x(step):
        for piece in range(X_PIECES):
            dispatch_x(piece, step, 0).wait_recv()
        forward_x(step, 0).start()

        @pl.when(step > 0)
        def _():
            for piece in range(X_PIECES):
                dispatch_x(piece, step, 1).wait_recv()

        forward_x(step, 1).start()

    diagonal = iota((cap, LANES), 0) == iota((cap, LANES), 1)

    def compute_x(step):
        for side in range(2):
            forward_x(step, side).wait_recv()
        gate_pre = jnp.zeros((4 * cap, half_width), F32)
        up_pre = jnp.zeros((4 * cap, half_width), F32)
        for piece in range(X_PIECES):
            block = r.xbuf[step, :, piece].reshape(8 * cap, x_wide)
            for part in range(2):
                start = (2 * piece + part) * x_wide
                columns = slice(start, start + x_wide)
                gate_pre = gate_pre + pick_rows(dot(block, r.gate_w[columns, :]), part)
                up_pre = up_pre + pick_rows(dot(block, r.up_w[columns, :]), part)
        hidden_grad = r.hidden_grad[step]
        logistic = jax.nn.sigmoid(gate_pre)
        activated = gate_pre * logistic
        share = jnp.sum(activated * up_pre * hidden_grad, axis=1, keepdims=True)
        for which in range(4):
            column = share[which * cap : (which + 1) * cap]
            line = jnp.sum(jnp.where(diagonal, column, 0.0), axis=0, keepdims=True)
            if which < 2:
                r.own_share[step, which] = line
            else:
                r.share_send[step, which - 2] = line
        partial_share(step).start()
        gate_grad = (
            hidden_grad * up_pre * logistic * (1.0 + gate_pre * (1.0 - logistic))
        ).astype(BF16)
        up_grad = (hidden_grad * activated).astype(BF16)
        chunk = min(512, width)
        for start in range(0, width, chunk):
            columns = slice(start, start + chunk)
            back = dot(gate_grad, r.gate_w[columns, :], (1, 1)) + dot(
                up_grad, r.up_w[columns, :], (1, 1)
            )
            r.own[step, :, columns] = back[: 2 * cap]
            r.psend[step, :, columns] = back[2 * cap :].astype(BF16)
        partial(step).start()

    def finish(step):
        partial_share(step).wait_recv()
        for side in range(2):
            r.ssend[step, side] = r.own_share[step, side] + r.share_recv[step, side]
        give_share(step, 0).start()

        @pl.when(step > 0)
        def _():
            give_share(step, 1).start()

        partial(step).wait_recv()
        total = r.own[step] + r.precv[step].astype(F32)
        stacked = []
        for side in range(2):
            mine = total[side * cap : (side + 1) * cap]
            stacked.append(jnp.concatenate([mine[:, :half_model], mine[:, half_model:]], axis=0))
            r.rsend[step, side] = stacked[side].astype(BF16)
        @pl.when(step < r_first)
        def _():
            give_back(step, 0).start()

        @pl.when((step > 0) & (step < r_first))
        def _():
            give_back(step, 1).start()

        give_gates(step, 0).wait_recv()

        @pl.when(step > 0)
        def _():
            give_gates(step, 1).wait_recv()

        for side in range(2):
            line = r.gate_in[step, side]
            column = jnp.sum(jnp.where(diagonal, line, 0.0), axis=1, keepdims=True)
            term = stacked[side] * r.xbuf[step, side, 0].astype(F32)
            for part in range(2):
                r.gain_sum[part : part + 1, :] += jnp.sum(
                    term[part * cap : (part + 1) * cap] * column, axis=0, keepdims=True
                )

    def pipeline_g(turn, carry):
        @pl.when(turn < steps)
        def _():
            receive_g(turn)

        @pl.when(turn >= 1)
        def _():
            compute_g(turn - 1)

        return carry

    def pipeline_x(turn, carry):
        @pl.when(turn < steps)
        def _():
            receive_x(turn)

        @pl.when((turn >= 1) & (turn <= steps))
        def _():
            compute_x(turn - 1)

        @pl.when(turn >= 2)
        def _():
            finish(turn - 2)

        return carry

    lax.fori_loop(0, steps + 1, pipeline_g, 0)
    lax.fori_loop(0, steps + 2, pipeline_x, 0)

    base = G_PIECES + X_PIECES
    self_back = pltpu.make_async_copy(r.rsend.at[0, 1], r.ret.at[chip], r.l_sem.at[base])
    self_share = pltpu.make_async_copy(r.ssend.at[0, 1], r.sret.at[chip], r.l_sem.at[base + 1])
    self_back.start()
    self_share.start()
    for block in range(blocks):
        part, column = divmod(block * LANES, half_model)
        r.y_src[block : block + 1, :] = r.gain_sum[part : part + 1, column : column + LANES]
    across_gain = remote(r.y_src, r.y_dst, (r.x_send, r.x_recv), 1, sibling)
    across_gain.start()
    self_share.wait()
    pairs(lambda step, side: give_share(step, side).wait_recv())

    shares = r.sret[...].reshape(nz, LANES)
    first, second = split(shares)
    third = (shares - first.astype(F32) - second.astype(F32)).astype(BF16)
    gate_share = []
    for k in range(2):
        onehot = jnp.where(expert_ids == picked[k], 1.0, 0.0).astype(BF16)
        line = dot(onehot, first) + dot(onehot, second) + dot(onehot, third)
        gate_share.append(
            jnp.sum(jnp.where(places == place_of[k], line, 0.0), axis=1, keepdims=True)
        )
    mean_share = gates[0] * gate_share[0] + gates[1] * gate_share[1]
    logit_grad = jnp.zeros((rows, nz), F32)
    for k in range(2):
        select_grad = gates[k] * (gate_share[k] - mean_share)
        logit_grad = logit_grad + jnp.where(expert_ids == picked[k], select_grad, 0.0)
    grad_high, grad_low = split(logit_grad)
    router_term = dot(grad_high, r.normed[...], (0, 0)) + dot(grad_low, r.normed[...], (0, 0))
    for block in range(blocks):
        r.stage[:, block, :] = router_term[:, block * LANES : (block + 1) * LANES]
    r.q_src[...] = r.stage[...].astype(BF16)
    others(lambda offset: reduce_router(offset).start())
    pairs(lambda step, side: give_back(step, side).start(), r_first, r_second)
    self_reduce = pltpu.make_async_copy(r.q_src.at[chip], r.q_dst.at[0], r.l_sem.at[base + 2])
    self_reduce.start()
    router_part = dot(grad_high, r.router_t[...]) + dot(grad_low, r.router_t[...])

    self_reduce.wait()
    others(lambda offset: reduce_router(offset).wait_recv())
    r.x_src[...] = jnp.sum(r.q_dst[...].astype(F32), axis=0)
    across_router = remote(r.x_src, r.x_dst, (r.x_send, r.x_recv), 0, sibling)
    across_router.start()

    across_gain.wait_recv()
    across_router.wait_recv()
    router_row = r.x_src[...] + r.x_dst[...]
    gain_row = r.y_src[...] + r.y_dst[...]
    mine = lax.rem(chip, 2) == core
    r.a_src[...] = jnp.where(mine, router_row, gain_row).astype(BF16)
    others(lambda offset: gather_router(offset).start())
    r.a_dst[chip] = r.a_src[...]

    pairs(lambda step, side: give_back(step, side).start(), r_second, steps)
    self_back.wait()
    pairs(lambda step, side: give_back(step, side).wait_recv())
    came_back = r.ret[...].reshape(nz * 2 * cap, half_model)
    both = dot(r.weights[...], came_back)
    normed_grad = jnp.concatenate([both[:rows], both[rows:]], axis=1) + router_part

    unit = sides(r.xex, X_PIECES).astype(F32) * inv
    scaled = normed_grad * r.gain[...].astype(F32)
    mean_scaled = jnp.mean(scaled * unit, axis=-1, keepdims=True)
    returned = sides(r.gex, G_PIECES).astype(F32)
    r.lig[...] = (returned + inv * (scaled - unit * mean_scaled)).astype(BF16)

    others(lambda offset: gather_router(offset).wait_recv())
    swap = remote(r.a_dst, r.b_dst, (r.x_send, r.x_recv), 2, sibling)
    swap.start()

    for piece in range(G_PIECES):
        for part in range(2):
            hand_back(part, piece).wait_send()
        pairs(lambda step, side, piece=piece: dispatch_g(piece, step, side).wait_send())
    for piece in range(X_PIECES):
        for part in range(2):
            hand_on(part, piece).wait_send()
        pairs(lambda step, side, piece=piece: dispatch_x(piece, step, side).wait_send())

    def drain(step, carry):
        for side in range(2):
            forward_g(step, side).wait_send()
            forward_x(step, side).wait_send()
        partial(step).wait_send()
        partial_share(step).wait_send()
        return carry

    lax.fori_loop(0, steps, drain, 0)
    pairs(lambda step, side: give_back(step, side).wait_send())
    pairs(lambda step, side: give_share(step, side).wait_send())
    others(lambda offset: reduce_router(offset).wait_send())
    others(lambda offset: gather_router(offset).wait_send())
    pairs(lambda step, side: give_gates(step, side).wait_send())
    across_router.wait_send()
    across_gain.wait_send()

    swap.wait()
    here = r.a_dst[...].astype(F32)
    there = r.b_dst[...].astype(F32)
    tall = here.shape[1]
    is_here = lax.rem(iota((nz, tall, LANES), 0), 2) == core
    router_rows = jnp.where(is_here, here, there)
    gain_rows = jnp.sum(jnp.where(is_here, there, here), axis=0)
    for block in range(blocks):
        columns = slice(block * LANES, (block + 1) * LANES)
        total = router_rows[:, block, :]
        r.router_total[:, columns] = total
        from_router = jnp.sum(total * r.router_t[:, columns].astype(F32), axis=0, keepdims=True)
        r.gain_total[:, columns] = (gain_rows[block : block + 1, :] + from_router) / r.gain[
            :, columns
        ].astype(F32)


def exchange(nz, cap, sections, lengths, picks, gain, router_t, acts, cots, gate, up, down):
    steps = nz // 2
    rows, width = acts.shape[1:]
    half_width = gate.shape[1]
    half_model = width // 2
    lines = width // LANES
    g_wide = half_model // G_PIECES
    x_wide = half_model // X_PIECES
    vmem = pl.BlockSpec(memory_space=pltpu.VMEM)
    anywhere = pl.BlockSpec(memory_space=pl.ANY)

    def sems(*shape):
        return pltpu.SemaphoreType.DMA(shape)

    tall = -(-lines // 16) * 16
    scratch = {
        "gate_w": pltpu.VMEM((width, half_width), BF16),
        "up_w": pltpu.VMEM((width, half_width), BF16),
        "down_w": pltpu.VMEM((half_width, width), BF16),
        "select": pltpu.VMEM((nz * 2 * cap, 2 * rows), BF16),
        "gex": pltpu.VMEM((G_PIECES, 2 * rows, g_wide), BF16),
        "xex": pltpu.VMEM((X_PIECES, 2 * rows, x_wide), BF16),
        "normed": pltpu.VMEM((rows, width), BF16),
        "dispg": pltpu.VMEM((G_PIECES, nz, 2 * cap, g_wide), BF16),
        "dispx": pltpu.VMEM((X_PIECES, nz, 2 * cap, x_wide), BF16),
        "gbuf": pltpu.VMEM((steps, 4, G_PIECES, 2 * cap, g_wide), BF16),
        "xbuf": pltpu.VMEM((steps, 4, X_PIECES, 2 * cap, x_wide), BF16),
        "hidden_grad": pltpu.VMEM((steps, 4 * cap, half_width), F32),
        "own": pltpu.VMEM((steps, 2 * cap, width), F32),
        "psend": pltpu.VMEM((steps, 2 * cap, width), BF16),
        "precv": pltpu.VMEM((steps, 2 * cap, width), BF16),
        "own_share": pltpu.VMEM((steps, 2, 1, LANES), F32),
        "share_send": pltpu.VMEM((steps, 2, 1, LANES), F32),
        "share_recv": pltpu.VMEM((steps, 2, 1, LANES), F32),
        "rsend": pltpu.VMEM((steps, 2, 2 * cap, half_model), BF16),
        "ret": pltpu.VMEM((nz, 2 * cap, half_model), BF16),
        "ssend": pltpu.VMEM((steps, 2, 1, LANES), F32),
        "sret": pltpu.VMEM((nz, 1, LANES), F32),
        "gate_out": pltpu.VMEM((nz, 1, LANES), F32),
        "gate_in": pltpu.VMEM((steps, 2, 1, LANES), F32),
        "gain_sum": pltpu.VMEM((2, half_model), F32),
        "weights": pltpu.VMEM((2 * rows, nz * 2 * cap), BF16),
        "stage": pltpu.VMEM((nz, tall, LANES), F32),
        "q_src": pltpu.VMEM((nz, tall, LANES), BF16),
        "q_dst": pltpu.VMEM((nz, tall, LANES), BF16),
        "x_src": pltpu.VMEM((tall, LANES), F32),
        "x_dst": pltpu.VMEM((tall, LANES), F32),
        "y_src": pltpu.VMEM((tall, LANES), F32),
        "y_dst": pltpu.VMEM((tall, LANES), F32),
        "a_src": pltpu.VMEM((tall, LANES), BF16),
        "a_dst": pltpu.VMEM((nz, tall, LANES), BF16),
        "b_dst": pltpu.VMEM((nz, tall, LANES), BF16),
        "w_sem": sems(3),
        "l_sem": sems(G_PIECES + X_PIECES + 3),
        "ge_send": sems(2 * G_PIECES),
        "ge_recv": sems(2 * G_PIECES),
        "xe_send": sems(2 * X_PIECES),
        "xe_recv": sems(2 * X_PIECES),
        "gd_send": sems(G_PIECES, steps, 2),
        "gd_recv": sems(G_PIECES, steps, 2),
        "xd_send": sems(X_PIECES, steps, 2),
        "xd_recv": sems(X_PIECES, steps, 2),
        "gf_send": sems(steps, 2),
        "gf_recv": sems(steps, 2),
        "xf_send": sems(steps, 2),
        "xf_recv": sems(steps, 2),
        "p_send": sems(steps),
        "p_recv": sems(steps),
        "h_send": sems(steps),
        "h_recv": sems(steps),
        "r_send": sems(steps, 2),
        "r_recv": sems(steps, 2),
        "s_send": sems(steps, 2),
        "s_recv": sems(steps, 2),
        "q_send": sems(nz),
        "q_recv": sems(nz),
        "x_send": sems(3),
        "x_recv": sems(3),
        "gg_send": sems(steps, 2),
        "gg_recv": sems(steps, 2),
        "a_send": sems(nz),
        "a_recv": sems(nz),
    }
    operands = ["lengths", "picks", "gain", "router_t", "acts", "cots"]
    operands += ["gate_hbm", "up_hbm", "down_hbm"]
    names = operands + ["lig", "router_total", "gain_total"] + list(scratch)
    return pl.pallas_call(
        functools.partial(kernel, nz, cap, sections, names),
        out_shape=(
            jax.ShapeDtypeStruct((rows, width), BF16),
            jax.ShapeDtypeStruct((nz, width), F32),
            jax.ShapeDtypeStruct((1, width), F32),
        ),
        in_specs=[vmem] * 4 + [anywhere] * 5,
        out_specs=(vmem, vmem, vmem),
        scratch_shapes=list(scratch.values()),
        compiler_params=pltpu.CompilerParams(
            collective_id=0, has_side_effects=True, vmem_limit_bytes=44 * 1024 * 1024
        ),
        cost_estimate=pl.CostEstimate(
            flops=8_000_000_000, bytes_accessed=8_000_000, transcendentals=200_000
        ),
    )(lengths, picks, gain, router_t, acts, cots, gate, up, down)


def per_device(
    activations,
    cotangents,
    norm_gain,
    routes,
    lengths,
    router_weight,
    gate_weight,
    up_weight,
    down_weight,
):
    rows, width = activations.shape[1:]
    experts = router_weight.shape[2]
    top = routes.shape[2]
    cap = 3 * rows * top // (2 * experts)
    lig, router_total, gain_total = exchange(
        experts,
        cap,
        lax.axis_size("section"),
        lengths,
        routes[0].T,
        norm_gain,
        router_weight[0].T,
        activations,
        cotangents,
        gate_weight[0, 0],
        up_weight[0, 0],
        down_weight[0, 0],
    )
    return (lig[None], router_total.T[None], gain_total)


def solution(mesh):
    in_specs = (
        P("section", "expert", None),
        P("section", "expert", None),
        P("section", None),
        P("section", "expert", None),
        P("section", "expert"),
        P("section", None, None),
        P("section", "expert", None, None),
        P("section", "expert", None, None),
        P("section", "expert", None, None),
    )
    out_specs = (P("section", "expert", None), P("section", None, None), P("section", None))
    return jax.shard_map(
        per_device, mesh=mesh, in_specs=in_specs, out_specs=out_specs, check_vma=False
    )
```

```python
import functools
import types

import jax
import jax.numpy as jnp
from jax import lax
from jax.experimental import pallas as pl
from jax.experimental.pallas import tpu as pltpu
from jax.sharding import PartitionSpec as P

EPSILON = 1e-05
LANES = 128
G_PIECES = 4
X_PIECES = 1
X_FIRST = 4
MESH = pl.DeviceIdType.MESH
F32 = jnp.float32
BF16 = jnp.bfloat16


def dot(a, b, contract=(1, 0)):
    return lax.dot_general(
        a, b, (((contract[0],), (contract[1],)), ((), ())), preferred_element_type=F32
    )


def split(value):
    high = value.astype(BF16)
    return high, (value - high.astype(F32)).astype(BF16)


def iota(shape, dim):
    return lax.broadcasted_iota(jnp.int32, shape, dim)


def kernel(nz, cap, sections, names, *refs):
    r = types.SimpleNamespace(**dict(zip(names, refs)))
    steps = nz // 2
    width, half_width = r.gate_w.shape
    half_model = width // 2
    rows = r.normed.shape[0]
    g_wide = half_model // G_PIECES
    x_wide = half_model // X_PIECES
    blocks = width // LANES
    r_first, r_second = steps // 2, 3 * steps // 4
    x_first = min(X_FIRST, steps)
    section = lax.axis_index("section")
    me = lax.axis_index("expert")
    chip = me // 2
    core = me - chip * 2
    sibling = chip * 2 + 1 - core
    section_before = lax.rem(section + sections - 1, sections)
    section_after = lax.rem(section + 1, sections)

    def at_offset(offset):
        return lax.rem(chip + offset + nz, nz) * 2 + core

    def remote(src, dst, sems, index, target, home=section):
        return pltpu.make_async_remote_copy(
            src_ref=src,
            dst_ref=dst,
            send_sem=sems[0].at[index],
            recv_sem=sems[1].at[index],
            device_id=(home, target),
            device_id_type=MESH,
        )

    def offset_of(step, side):
        return steps - step if side == 0 else lax.rem(steps + step, nz)

    def hand_on(part, piece):
        columns = pl.ds((2 * piece + part) * x_wide, x_wide)
        return remote(
            r.acts.at[0, :, columns],
            r.xex.at[piece, pl.ds(part * rows, rows), :],
            (r.xe_send, r.xe_recv),
            2 * piece + part,
            me,
            section_after,
        )

    def hand_back(part, piece):
        columns = pl.ds((2 * piece + part) * g_wide, g_wide)
        return remote(
            r.cots.at[0, :, columns],
            r.gex.at[piece, pl.ds(part * rows, rows), :],
            (r.ge_send, r.ge_recv),
            2 * piece + part,
            me,
            section_before,
        )

    def dispatch_g(piece, step, side):
        target = at_offset(offset_of(step, side))
        return remote(
            r.dispg.at[piece, target // 2],
            r.gbuf.at[step, side, piece],
            (r.gd_send, r.gd_recv),
            (piece, step, side),
            target,
        )

    def dispatch_x(piece, step, side):
        target = at_offset(offset_of(step, side))
        return remote(
            r.dispx.at[piece, target // 2],
            r.xbuf.at[step, side, piece],
            (r.xd_send, r.xd_recv),
            (piece, step, side),
            target,
        )

    def forward_g(step, side):
        return remote(
            r.gbuf.at[step, side],
            r.gbuf.at[step, 2 + side],
            (r.gf_send, r.gf_recv),
            (step, side),
            sibling,
        )

    def forward_x(step, side):
        return remote(
            r.xbuf.at[step, side],
            r.xbuf.at[step, 2 + side],
            (r.xf_send, r.xf_recv),
            (step, side),
            sibling,
        )

    def partial(step):
        return remote(r.psend.at[step], r.precv.at[step], (r.p_send, r.p_recv), step, sibling)

    def partial_share(step):
        return remote(
            r.share_send.at[step], r.share_recv.at[step], (r.h_send, r.h_recv), step, sibling
        )

    def give_back(step, side):
        target = at_offset(-offset_of(step, side))
        return remote(
            r.rsend.at[step, side], r.ret.at[chip], (r.r_send, r.r_recv), (step, side), target
        )

    def give_share(step, side):
        target = at_offset(-offset_of(step, side))
        return remote(
            r.ssend.at[step, side], r.sret.at[chip], (r.s_send, r.s_recv), (step, side), target
        )

    def give_gates(step, side):
        target = at_offset(offset_of(step, side))
        return remote(
            r.gate_out.at[target // 2],
            r.gate_in.at[step, side],
            (r.gg_send, r.gg_recv),
            (step, side),
            target,
        )

    def reduce_router(offset):
        target = at_offset(offset)
        return remote(
            r.q_src.at[target // 2], r.q_dst.at[offset], (r.q_send, r.q_recv), offset, target
        )

    def gather_router(offset):
        return remote(
            r.a_src, r.a_dst.at[chip], (r.a_send, r.a_recv), offset, at_offset(offset)
        )

    def pairs(body, first=0, last=steps):
        def both(step, carry):
            body(step, 0)

            @pl.when(step > 0)
            def _():
                body(step, 1)

            return carry

        lax.fori_loop(first, last, both, 0)

    def others(body):
        def one(offset, carry):
            body(offset)
            return carry

        lax.fori_loop(1, nz, one, 0)

    barrier = pltpu.get_barrier_semaphore()

    def greet(offset):
        pl.semaphore_signal(
            barrier, inc=1, device_id=(section, at_offset(offset)), device_id_type=MESH
        )

    others(greet)
    for home, target in ((section, sibling), (section_before, me), (section_after, me)):
        pl.semaphore_signal(barrier, inc=1, device_id=(home, target), device_id_type=MESH)
    loads = [
        pltpu.make_async_copy(r.gate_hbm, r.gate_w, r.w_sem.at[0]),
        pltpu.make_async_copy(r.up_hbm, r.up_w, r.w_sem.at[1]),
        pltpu.make_async_copy(r.down_hbm, r.down_w, r.w_sem.at[2]),
    ]
    for load in loads:
        load.start()

    live = iota((1, rows), 1) < r.lengths[...]
    named = [iota((nz, rows), 0) == r.picks[k : k + 1, :] for k in range(2)]
    hot = jnp.where((named[0] | named[1]) & live, 1.0, 0.0).astype(BF16)
    earlier = jnp.where(iota((rows, rows), 0) < iota((rows, rows), 1), 1.0, 0.0).astype(BF16)
    before = dot(hot, earlier)
    targets = []
    for k in range(2):
        place = jnp.sum(jnp.where(named[k], before, 0.0), axis=0, keepdims=True)
        slot = r.picks[k : k + 1, :] * (2 * cap) + place.astype(jnp.int32)
        targets.append(jnp.where(live, slot, -4 * cap))
    slots = iota((nz * 2 * cap, rows), 0)
    for part in range(2):
        chosen = (slots == targets[0] + part * cap) | (slots == targets[1] + part * cap)
        r.select[:, part * rows : (part + 1) * rows] = jnp.where(chosen, 1.0, 0.0).astype(BF16)

    pl.semaphore_wait(barrier, nz + 2)

    for piece in range(G_PIECES):
        for part in range(2):
            hand_back(part, piece).start()
    for piece in range(X_PIECES):
        for part in range(2):
            hand_on(part, piece).start()

    own_copies = []
    for piece in range(G_PIECES):
        for part in range(2):
            hand_back(part, piece).wait_recv()
        spread = dot(r.select[...], r.gex[piece]).astype(BF16)
        r.dispg[piece] = spread.reshape(nz, 2 * cap, g_wide)
        pairs(lambda step, side, piece=piece: dispatch_g(piece, step, side).start())
        own_copies.append(
            pltpu.make_async_copy(
                r.dispg.at[piece, chip], r.gbuf.at[0, 1, piece], r.l_sem.at[len(own_copies)]
            )
        )
        own_copies[-1].start()

    for piece in range(X_PIECES):
        for part in range(2):
            hand_on(part, piece).wait_recv()

    def sides(ref, count):
        parts = [
            ref[piece, part * rows : (part + 1) * rows, :]
            for piece in range(count)
            for part in range(2)
        ]
        return jnp.concatenate(parts, axis=1)

    full = sides(r.xex, X_PIECES).astype(F32)
    inv = lax.rsqrt(jnp.mean(full * full, axis=-1, keepdims=True) + EPSILON)
    r.normed[...] = (full * inv * r.gain[...].astype(F32)).astype(BF16)
    for piece in range(X_PIECES):
        start = 2 * piece * x_wide
        both = jnp.concatenate(
            [r.normed[:, start : start + x_wide], r.normed[:, start + x_wide : start + 2 * x_wide]],
            axis=0,
        )
        spread = dot(r.select[...], both).astype(BF16)
        r.dispx[piece] = spread.reshape(nz, 2 * cap, x_wide)
        pairs(
            lambda step, side, piece=piece: dispatch_x(piece, step, side).start(), 0, x_first
        )
        own_copies.append(
            pltpu.make_async_copy(
                r.dispx.at[piece, chip], r.xbuf.at[0, 1, piece], r.l_sem.at[len(own_copies)]
            )
        )
        own_copies[-1].start()

    same = iota((rows, rows), 0) == iota((rows, rows), 1)

    def upright(line):
        return jnp.sum(jnp.where(same, line, 0), axis=1, keepdims=True)

    expert_ids = iota((rows, nz), 1)
    picked = [upright(r.picks[k : k + 1, :]) for k in range(2)]
    target_of = [upright(targets[k]) for k in range(2)]
    logits = dot(r.normed[...], r.router_t[...], (1, 1))
    scores = [
        jnp.sum(jnp.where(expert_ids == picked[k], logits, 0.0), axis=1, keepdims=True)
        for k in range(2)
    ]
    gates = [1.0 / (1.0 + jnp.exp(scores[1 - k] - scores[k])) for k in range(2)]
    places = iota((rows, LANES), 1)
    place_of = [target_of[k] - picked[k] * (2 * cap) for k in range(2)]
    slot_gates = jnp.zeros((nz, LANES), F32)
    for k in range(2):
        onehot = jnp.where(named[k], 1.0, 0.0).astype(BF16)
        for piece in split(jnp.where(places == place_of[k], gates[k], 0.0)):
            slot_gates = slot_gates + dot(onehot, piece)
    r.gate_out[...] = slot_gates.reshape(nz, 1, LANES)
    pairs(lambda step, side: give_gates(step, side).start())
    r.gate_in[0, 1] = r.gate_out[chip]
    r.gain_sum[...] = jnp.zeros_like(r.gain_sum)
    across_slots = iota((rows, nz * 2 * cap), 1)
    for part in range(2):
        mix = jnp.where(across_slots == target_of[0] + part * cap, gates[0], 0.0)
        mix = mix + jnp.where(across_slots == target_of[1] + part * cap, gates[1], 0.0)
        r.weights[part * rows : (part + 1) * rows, :] = mix.astype(BF16)

    for copy in own_copies:
        copy.wait()
    for load in loads:
        load.wait()

    def pick_rows(value, part):
        return value.reshape(4, 2 * cap, half_width)[:, part * cap : (part + 1) * cap].reshape(
            4 * cap, half_width
        )

    def receive_g(step):
        for piece in range(G_PIECES):
            dispatch_g(piece, step, 0).wait_recv()
        forward_g(step, 0).start()

        @pl.when(step > 0)
        def _():
            for piece in range(G_PIECES):
                dispatch_g(piece, step, 1).wait_recv()

        forward_g(step, 1).start()

    def compute_g(step):
        for side in range(2):
            forward_g(step, side).wait_recv()
        total = jnp.zeros((4 * cap, half_width), F32)
        for piece in range(G_PIECES):
            block = r.gbuf[step, :, piece].reshape(8 * cap, g_wide)
            for part in range(2):
                start = (2 * piece + part) * g_wide
                down = r.down_w[:, start : start + g_wide]
                total = total + pick_rows(dot(block, down, (1, 1)), part)
        r.hidden_grad[step] = total

    def receive_x(step):
        for piece in range(X_PIECES):
            dispatch_x(piece, step, 0).wait_recv()
        forward_x(step, 0).start()

        @pl.when(step > 0)
        def _():
            for piece in range(X_PIECES):
                dispatch_x(piece, step, 1).wait_recv()

        forward_x(step, 1).start()

    diagonal = iota((cap, LANES), 0) == iota((cap, LANES), 1)

    def compute_x(step):
        for side in range(2):
            forward_x(step, side).wait_recv()
        gate_pre = jnp.zeros((4 * cap, half_width), F32)
        up_pre = jnp.zeros((4 * cap, half_width), F32)
        for piece in range(X_PIECES):
            block = r.xbuf[step, :, piece].reshape(8 * cap, x_wide)
            for part in range(2):
                start = (2 * piece + part) * x_wide
                columns = slice(start, start + x_wide)
                gate_pre = gate_pre + pick_rows(dot(block, r.gate_w[columns, :]), part)
                up_pre = up_pre + pick_rows(dot(block, r.up_w[columns, :]), part)
        hidden_grad = r.hidden_grad[step]
        logistic = jax.nn.sigmoid(gate_pre)
        activated = gate_pre * logistic
        share = jnp.sum(activated * up_pre * hidden_grad, axis=1, keepdims=True)
        for which in range(4):
            column = share[which * cap : (which + 1) * cap]
            line = jnp.sum(jnp.where(diagonal, column, 0.0), axis=0, keepdims=True)
            if which < 2:
                r.own_share[step, which] = line
            else:
                r.share_send[step, which - 2] = line
        partial_share(step).start()
        gate_grad = (
            hidden_grad * up_pre * logistic * (1.0 + gate_pre * (1.0 - logistic))
        ).astype(BF16)
        up_grad = (hidden_grad * activated).astype(BF16)
        chunk = min(512, width)
        for start in range(0, width, chunk):
            columns = slice(start, start + chunk)
            back = dot(gate_grad, r.gate_w[columns, :], (1, 1)) + dot(
                up_grad, r.up_w[columns, :], (1, 1)
            )
            r.own[step, :, columns] = back[: 2 * cap]
            r.psend[step, :, columns] = back[2 * cap :].astype(BF16)
        partial(step).start()

    def finish(step):
        partial_share(step).wait_recv()
        for side in range(2):
            r.ssend[step, side] = r.own_share[step, side] + r.share_recv[step, side]
        give_share(step, 0).start()

        @pl.when(step > 0)
        def _():
            give_share(step, 1).start()

        partial(step).wait_recv()
        total = r.own[step] + r.precv[step].astype(F32)
        stacked = []
        for side in range(2):
            mine = total[side * cap : (side + 1) * cap]
            stacked.append(jnp.concatenate([mine[:, :half_model], mine[:, half_model:]], axis=0))
            r.rsend[step, side] = stacked[side].astype(BF16)
        @pl.when(step < r_first)
        def _():
            give_back(step, 0).start()

        @pl.when((step > 0) & (step < r_first))
        def _():
            give_back(step, 1).start()

        give_gates(step, 0).wait_recv()

        @pl.when(step > 0)
        def _():
            give_gates(step, 1).wait_recv()

        for side in range(2):
            line = r.gate_in[step, side]
            column = jnp.sum(jnp.where(diagonal, line, 0.0), axis=1, keepdims=True)
            term = stacked[side] * r.xbuf[step, side, 0].astype(F32)
            for part in range(2):
                r.gain_sum[part : part + 1, :] += jnp.sum(
                    term[part * cap : (part + 1) * cap] * column, axis=0, keepdims=True
                )

    def pipeline_g(turn, carry):
        @pl.when(turn < steps)
        def _():
            receive_g(turn)

        @pl.when(turn >= 1)
        def _():
            compute_g(turn - 1)

        return carry

    def pipeline_x(turn, carry):
        @pl.when(turn < steps)
        def _():
            receive_x(turn)

        @pl.when(turn < steps - x_first)
        def _():
            for piece in range(X_PIECES):
                for side in range(2):
                    dispatch_x(piece, turn + x_first, side).start()

        @pl.when((turn >= 1) & (turn <= steps))
        def _():
            compute_x(turn - 1)

        @pl.when(turn >= 2)
        def _():
            finish(turn - 2)

        return carry

    lax.fori_loop(0, steps + 1, pipeline_g, 0)
    lax.fori_loop(0, steps + 2, pipeline_x, 0)

    base = G_PIECES + X_PIECES
    self_back = pltpu.make_async_copy(r.rsend.at[0, 1], r.ret.at[chip], r.l_sem.at[base])
    self_share = pltpu.make_async_copy(r.ssend.at[0, 1], r.sret.at[chip], r.l_sem.at[base + 1])
    self_back.start()
    self_share.start()
    for block in range(blocks):
        part, column = divmod(block * LANES, half_model)
        r.y_src[block : block + 1, :] = r.gain_sum[part : part + 1, column : column + LANES]
    across_gain = remote(r.y_src, r.y_dst, (r.x_send, r.x_recv), 1, sibling)
    across_gain.start()
    self_share.wait()
    pairs(lambda step, side: give_share(step, side).wait_recv())

    shares = r.sret[...].reshape(nz, LANES)
    first, second = split(shares)
    third = (shares - first.astype(F32) - second.astype(F32)).astype(BF16)
    gate_share = []
    for k in range(2):
        onehot = jnp.where(expert_ids == picked[k], 1.0, 0.0).astype(BF16)
        line = dot(onehot, first) + dot(onehot, second) + dot(onehot, third)
        gate_share.append(
            jnp.sum(jnp.where(places == place_of[k], line, 0.0), axis=1, keepdims=True)
        )
    mean_share = gates[0] * gate_share[0] + gates[1] * gate_share[1]
    logit_grad = jnp.zeros((rows, nz), F32)
    for k in range(2):
        select_grad = gates[k] * (gate_share[k] - mean_share)
        logit_grad = logit_grad + jnp.where(expert_ids == picked[k], select_grad, 0.0)
    grad_high, grad_low = split(logit_grad)
    router_term = dot(grad_high, r.normed[...], (0, 0)) + dot(grad_low, r.normed[...], (0, 0))
    for block in range(blocks):
        r.stage[:, block, :] = router_term[:, block * LANES : (block + 1) * LANES]
    r.q_src[...] = r.stage[...].astype(BF16)
    others(lambda offset: reduce_router(offset).start())
    pairs(lambda step, side: give_back(step, side).start(), r_first, r_second)
    self_reduce = pltpu.make_async_copy(r.q_src.at[chip], r.q_dst.at[0], r.l_sem.at[base + 2])
    self_reduce.start()
    router_part = dot(grad_high, r.router_t[...]) + dot(grad_low, r.router_t[...])

    self_reduce.wait()
    others(lambda offset: reduce_router(offset).wait_recv())
    r.x_src[...] = jnp.sum(r.q_dst[...].astype(F32), axis=0)
    across_router = remote(r.x_src, r.x_dst, (r.x_send, r.x_recv), 0, sibling)
    across_router.start()

    across_gain.wait_recv()
    across_router.wait_recv()
    router_row = r.x_src[...] + r.x_dst[...]
    gain_row = r.y_src[...] + r.y_dst[...]
    mine = lax.rem(chip, 2) == core
    r.a_src[...] = jnp.where(mine, router_row, gain_row).astype(BF16)
    others(lambda offset: gather_router(offset).start())
    r.a_dst[chip] = r.a_src[...]

    pairs(lambda step, side: give_back(step, side).start(), r_second, steps)
    self_back.wait()
    pairs(lambda step, side: give_back(step, side).wait_recv())
    came_back = r.ret[...].reshape(nz * 2 * cap, half_model)
    both = dot(r.weights[...], came_back)
    normed_grad = jnp.concatenate([both[:rows], both[rows:]], axis=1) + router_part

    unit = sides(r.xex, X_PIECES).astype(F32) * inv
    scaled = normed_grad * r.gain[...].astype(F32)
    mean_scaled = jnp.mean(scaled * unit, axis=-1, keepdims=True)
    returned = sides(r.gex, G_PIECES).astype(F32)
    r.lig[...] = (returned + inv * (scaled - unit * mean_scaled)).astype(BF16)

    others(lambda offset: gather_router(offset).wait_recv())
    swap = remote(r.a_dst, r.b_dst, (r.x_send, r.x_recv), 2, sibling)
    swap.start()

    for piece in range(G_PIECES):
        for part in range(2):
            hand_back(part, piece).wait_send()
        pairs(lambda step, side, piece=piece: dispatch_g(piece, step, side).wait_send())
    for piece in range(X_PIECES):
        for part in range(2):
            hand_on(part, piece).wait_send()
        pairs(lambda step, side, piece=piece: dispatch_x(piece, step, side).wait_send())

    def drain(step, carry):
        for side in range(2):
            forward_g(step, side).wait_send()
            forward_x(step, side).wait_send()
        partial(step).wait_send()
        partial_share(step).wait_send()
        return carry

    lax.fori_loop(0, steps, drain, 0)
    pairs(lambda step, side: give_back(step, side).wait_send())
    pairs(lambda step, side: give_share(step, side).wait_send())
    others(lambda offset: reduce_router(offset).wait_send())
    others(lambda offset: gather_router(offset).wait_send())
    pairs(lambda step, side: give_gates(step, side).wait_send())
    across_router.wait_send()
    across_gain.wait_send()

    swap.wait()
    here = r.a_dst[...].astype(F32)
    there = r.b_dst[...].astype(F32)
    tall = here.shape[1]
    is_here = lax.rem(iota((nz, tall, LANES), 0), 2) == core
    router_rows = jnp.where(is_here, here, there)
    gain_rows = jnp.sum(jnp.where(is_here, there, here), axis=0)
    for block in range(blocks):
        columns = slice(block * LANES, (block + 1) * LANES)
        total = router_rows[:, block, :]
        r.router_total[:, columns] = total
        from_router = jnp.sum(total * r.router_t[:, columns].astype(F32), axis=0, keepdims=True)
        r.gain_total[:, columns] = (gain_rows[block : block + 1, :] + from_router) / r.gain[
            :, columns
        ].astype(F32)


def exchange(nz, cap, sections, lengths, picks, gain, router_t, acts, cots, gate, up, down):
    steps = nz // 2
    rows, width = acts.shape[1:]
    half_width = gate.shape[1]
    half_model = width // 2
    lines = width // LANES
    g_wide = half_model // G_PIECES
    x_wide = half_model // X_PIECES
    vmem = pl.BlockSpec(memory_space=pltpu.VMEM)
    anywhere = pl.BlockSpec(memory_space=pl.ANY)

    def sems(*shape):
        return pltpu.SemaphoreType.DMA(shape)

    tall = -(-lines // 16) * 16
    scratch = {
        "gate_w": pltpu.VMEM((width, half_width), BF16),
        "up_w": pltpu.VMEM((width, half_width), BF16),
        "down_w": pltpu.VMEM((half_width, width), BF16),
        "select": pltpu.VMEM((nz * 2 * cap, 2 * rows), BF16),
        "gex": pltpu.VMEM((G_PIECES, 2 * rows, g_wide), BF16),
        "xex": pltpu.VMEM((X_PIECES, 2 * rows, x_wide), BF16),
        "normed": pltpu.VMEM((rows, width), BF16),
        "dispg": pltpu.VMEM((G_PIECES, nz, 2 * cap, g_wide), BF16),
        "dispx": pltpu.VMEM((X_PIECES, nz, 2 * cap, x_wide), BF16),
        "gbuf": pltpu.VMEM((steps, 4, G_PIECES, 2 * cap, g_wide), BF16),
        "xbuf": pltpu.VMEM((steps, 4, X_PIECES, 2 * cap, x_wide), BF16),
        "hidden_grad": pltpu.VMEM((steps, 4 * cap, half_width), F32),
        "own": pltpu.VMEM((steps, 2 * cap, width), F32),
        "psend": pltpu.VMEM((steps, 2 * cap, width), BF16),
        "precv": pltpu.VMEM((steps, 2 * cap, width), BF16),
        "own_share": pltpu.VMEM((steps, 2, 1, LANES), F32),
        "share_send": pltpu.VMEM((steps, 2, 1, LANES), F32),
        "share_recv": pltpu.VMEM((steps, 2, 1, LANES), F32),
        "rsend": pltpu.VMEM((steps, 2, 2 * cap, half_model), BF16),
        "ret": pltpu.VMEM((nz, 2 * cap, half_model), BF16),
        "ssend": pltpu.VMEM((steps, 2, 1, LANES), F32),
        "sret": pltpu.VMEM((nz, 1, LANES), F32),
        "gate_out": pltpu.VMEM((nz, 1, LANES), F32),
        "gate_in": pltpu.VMEM((steps, 2, 1, LANES), F32),
        "gain_sum": pltpu.VMEM((2, half_model), F32),
        "weights": pltpu.VMEM((2 * rows, nz * 2 * cap), BF16),
        "stage": pltpu.VMEM((nz, tall, LANES), F32),
        "q_src": pltpu.VMEM((nz, tall, LANES), BF16),
        "q_dst": pltpu.VMEM((nz, tall, LANES), BF16),
        "x_src": pltpu.VMEM((tall, LANES), F32),
        "x_dst": pltpu.VMEM((tall, LANES), F32),
        "y_src": pltpu.VMEM((tall, LANES), F32),
        "y_dst": pltpu.VMEM((tall, LANES), F32),
        "a_src": pltpu.VMEM((tall, LANES), BF16),
        "a_dst": pltpu.VMEM((nz, tall, LANES), BF16),
        "b_dst": pltpu.VMEM((nz, tall, LANES), BF16),
        "w_sem": sems(3),
        "l_sem": sems(G_PIECES + X_PIECES + 3),
        "ge_send": sems(2 * G_PIECES),
        "ge_recv": sems(2 * G_PIECES),
        "xe_send": sems(2 * X_PIECES),
        "xe_recv": sems(2 * X_PIECES),
        "gd_send": sems(G_PIECES, steps, 2),
        "gd_recv": sems(G_PIECES, steps, 2),
        "xd_send": sems(X_PIECES, steps, 2),
        "xd_recv": sems(X_PIECES, steps, 2),
        "gf_send": sems(steps, 2),
        "gf_recv": sems(steps, 2),
        "xf_send": sems(steps, 2),
        "xf_recv": sems(steps, 2),
        "p_send": sems(steps),
        "p_recv": sems(steps),
        "h_send": sems(steps),
        "h_recv": sems(steps),
        "r_send": sems(steps, 2),
        "r_recv": sems(steps, 2),
        "s_send": sems(steps, 2),
        "s_recv": sems(steps, 2),
        "q_send": sems(nz),
        "q_recv": sems(nz),
        "x_send": sems(3),
        "x_recv": sems(3),
        "gg_send": sems(steps, 2),
        "gg_recv": sems(steps, 2),
        "a_send": sems(nz),
        "a_recv": sems(nz),
    }
    operands = ["lengths", "picks", "gain", "router_t", "acts", "cots"]
    operands += ["gate_hbm", "up_hbm", "down_hbm"]
    names = operands + ["lig", "router_total", "gain_total"] + list(scratch)
    return pl.pallas_call(
        functools.partial(kernel, nz, cap, sections, names),
        out_shape=(
            jax.ShapeDtypeStruct((rows, width), BF16),
            jax.ShapeDtypeStruct((nz, width), F32),
            jax.ShapeDtypeStruct((1, width), F32),
        ),
        in_specs=[vmem] * 4 + [anywhere] * 5,
        out_specs=(vmem, vmem, vmem),
        scratch_shapes=list(scratch.values()),
        compiler_params=pltpu.CompilerParams(
            collective_id=0, has_side_effects=True, vmem_limit_bytes=44 * 1024 * 1024
        ),
        cost_estimate=pl.CostEstimate(
            flops=8_000_000_000, bytes_accessed=8_000_000, transcendentals=200_000
        ),
    )(lengths, picks, gain, router_t, acts, cots, gate, up, down)


def per_device(
    activations,
    cotangents,
    norm_gain,
    routes,
    lengths,
    router_weight,
    gate_weight,
    up_weight,
    down_weight,
):
    rows, width = activations.shape[1:]
    experts = router_weight.shape[2]
    top = routes.shape[2]
    cap = 3 * rows * top // (2 * experts)
    lig, router_total, gain_total = exchange(
        experts,
        cap,
        lax.axis_size("section"),
        lengths,
        routes[0].T,
        norm_gain,
        router_weight[0].T,
        activations,
        cotangents,
        gate_weight[0, 0],
        up_weight[0, 0],
        down_weight[0, 0],
    )
    return (lig[None], router_total.T[None], gain_total)


def solution(mesh):
    in_specs = (
        P("section", "expert", None),
        P("section", "expert", None),
        P("section", None),
        P("section", "expert", None),
        P("section", "expert"),
        P("section", None, None),
        P("section", "expert", None, None),
        P("section", "expert", None, None),
        P("section", "expert", None, None),
    )
    out_specs = (P("section", "expert", None), P("section", None, None), P("section", None))
    return jax.shard_map(
        per_device, mesh=mesh, in_specs=in_specs, out_specs=out_specs, check_vma=False
    )
```

```python
import functools
import types

import jax
import jax.numpy as jnp
from jax import lax
from jax.experimental import pallas as pl
from jax.experimental.pallas import tpu as pltpu
from jax.sharding import PartitionSpec as P

EPSILON = 1e-05
LANES = 128
G_PIECES = 4
X_PIECES = 1
X_FIRST = 4
MESH = pl.DeviceIdType.MESH
F32 = jnp.float32
BF16 = jnp.bfloat16


def dot(a, b, contract=(1, 0)):
    return lax.dot_general(
        a, b, (((contract[0],), (contract[1],)), ((), ())), preferred_element_type=F32
    )


def split(value):
    high = value.astype(BF16)
    return high, (value - high.astype(F32)).astype(BF16)


def iota(shape, dim):
    return lax.broadcasted_iota(jnp.int32, shape, dim)


def kernel(nz, cap, sections, names, *refs):
    r = types.SimpleNamespace(**dict(zip(names, refs)))
    steps = nz // 2
    width, half_width = r.gate_w.shape
    half_model = width // 2
    rows = r.normed.shape[0]
    g_wide = half_model // G_PIECES
    x_wide = half_model // X_PIECES
    blocks = width // LANES
    r_first, r_second = steps // 2, 3 * steps // 4
    x_first = min(X_FIRST, steps)
    section = lax.axis_index("section")
    me = lax.axis_index("expert")
    chip = me // 2
    core = me - chip * 2
    sibling = chip * 2 + 1 - core
    section_before = lax.rem(section + sections - 1, sections)
    section_after = lax.rem(section + 1, sections)

    def at_offset(offset):
        return lax.rem(chip + offset + nz, nz) * 2 + core

    def remote(src, dst, sems, index, target, home=section):
        return pltpu.make_async_remote_copy(
            src_ref=src,
            dst_ref=dst,
            send_sem=sems[0].at[index],
            recv_sem=sems[1].at[index],
            device_id=(home, target),
            device_id_type=MESH,
        )

    def offset_of(step, side):
        return steps - step if side == 0 else lax.rem(steps + step, nz)

    def hand_on(part, piece):
        columns = pl.ds((2 * piece + part) * x_wide, x_wide)
        return remote(
            r.acts.at[0, :, columns],
            r.xex.at[piece, pl.ds(part * rows, rows), :],
            (r.xe_send, r.xe_recv),
            2 * piece + part,
            me,
            section_after,
        )

    def hand_back(part, piece):
        columns = pl.ds((2 * piece + part) * g_wide, g_wide)
        return remote(
            r.cots.at[0, :, columns],
            r.gex.at[piece, pl.ds(part * rows, rows), :],
            (r.ge_send, r.ge_recv),
            2 * piece + part,
            me,
            section_before,
        )

    def dispatch_g(piece, step, side):
        target = at_offset(offset_of(step, side))
        return remote(
            r.dispg.at[piece, target // 2],
            r.gbuf.at[step, side, piece],
            (r.gd_send, r.gd_recv),
            (piece, step, side),
            target,
        )

    def dispatch_x(piece, step, side):
        target = at_offset(offset_of(step, side))
        return remote(
            r.dispx.at[piece, target // 2],
            r.xbuf.at[step, side, piece],
            (r.xd_send, r.xd_recv),
            (piece, step, side),
            target,
        )

    def forward_g(step, side):
        return remote(
            r.gbuf.at[step, side],
            r.gbuf.at[step, 2 + side],
            (r.gf_send, r.gf_recv),
            (step, side),
            sibling,
        )

    def forward_x(step, side):
        return remote(
            r.xbuf.at[step, side],
            r.xbuf.at[step, 2 + side],
            (r.xf_send, r.xf_recv),
            (step, side),
            sibling,
        )

    def partial(step):
        return remote(r.psend.at[step], r.precv.at[step], (r.p_send, r.p_recv), step, sibling)

    def partial_share(step):
        return remote(
            r.share_send.at[step], r.share_recv.at[step], (r.h_send, r.h_recv), step, sibling
        )

    def give_back(step, side):
        target = at_offset(-offset_of(step, side))
        return remote(
            r.rsend.at[step, side], r.ret.at[chip], (r.r_send, r.r_recv), (step, side), target
        )

    def give_share(step, side):
        target = at_offset(-offset_of(step, side))
        return remote(
            r.ssend.at[step, side], r.sret.at[chip], (r.s_send, r.s_recv), (step, side), target
        )

    def give_gates(step, side):
        target = at_offset(offset_of(step, side))
        return remote(
            r.gate_out.at[target // 2],
            r.gate_in.at[step, side],
            (r.gg_send, r.gg_recv),
            (step, side),
            target,
        )

    def reduce_router(offset):
        target = at_offset(offset)
        return remote(
            r.q_src.at[target // 2], r.q_dst.at[offset], (r.q_send, r.q_recv), offset, target
        )

    def gather_router(offset):
        return remote(
            r.a_src, r.a_dst.at[chip], (r.a_send, r.a_recv), offset, at_offset(offset)
        )

    def pairs(body, first=0, last=steps):
        def both(step, carry):
            body(step, 0)

            @pl.when(step > 0)
            def _():
                body(step, 1)

            return carry

        lax.fori_loop(first, last, both, 0)

    def others(body):
        def one(offset, carry):
            body(offset)
            return carry

        lax.fori_loop(1, nz, one, 0)

    barrier = pltpu.get_barrier_semaphore()

    def greet(offset):
        pl.semaphore_signal(
            barrier, inc=1, device_id=(section, at_offset(offset)), device_id_type=MESH
        )

    others(greet)
    for home, target in ((section, sibling), (section_before, me), (section_after, me)):
        pl.semaphore_signal(barrier, inc=1, device_id=(home, target), device_id_type=MESH)
    loads = [
        pltpu.make_async_copy(r.gate_hbm, r.gate_w, r.w_sem.at[0]),
        pltpu.make_async_copy(r.up_hbm, r.up_w, r.w_sem.at[1]),
        pltpu.make_async_copy(r.down_hbm, r.down_w, r.w_sem.at[2]),
    ]
    for load in loads:
        load.start()

    live = iota((1, rows), 1) < r.lengths[...]
    named = [iota((nz, rows), 0) == r.picks[k : k + 1, :] for k in range(2)]
    hot = jnp.where((named[0] | named[1]) & live, 1.0, 0.0).astype(BF16)
    earlier = jnp.where(iota((rows, rows), 0) < iota((rows, rows), 1), 1.0, 0.0).astype(BF16)
    before = dot(hot, earlier)
    targets = []
    for k in range(2):
        place = jnp.sum(jnp.where(named[k], before, 0.0), axis=0, keepdims=True)
        slot = r.picks[k : k + 1, :] * (2 * cap) + place.astype(jnp.int32)
        targets.append(jnp.where(live, slot, -4 * cap))
    slots = iota((nz * 2 * cap, rows), 0)
    for part in range(2):
        chosen = (slots == targets[0] + part * cap) | (slots == targets[1] + part * cap)
        r.select[:, part * rows : (part + 1) * rows] = jnp.where(chosen, 1.0, 0.0).astype(BF16)

    pl.semaphore_wait(barrier, nz + 2)

    for part in range(2):
        hand_back(part, 0).start()
    own_copies = []
    for piece in range(G_PIECES):
        for part in range(2):
            hand_back(part, piece).wait_recv()
        if piece + 1 < G_PIECES:
            for part in range(2):
                hand_back(part, piece + 1).start()
        spread = dot(r.select[...], r.gex[piece]).astype(BF16)
        r.dispg[piece] = spread.reshape(nz, 2 * cap, g_wide)
        pairs(lambda step, side, piece=piece: dispatch_g(piece, step, side).start())
        own_copies.append(
            pltpu.make_async_copy(
                r.dispg.at[piece, chip], r.gbuf.at[0, 1, piece], r.l_sem.at[len(own_copies)]
            )
        )
        own_copies[-1].start()
        if piece == G_PIECES // 2 - 1:
            for x_piece in range(X_PIECES):
                for part in range(2):
                    hand_on(part, x_piece).start()

    for piece in range(X_PIECES):
        for part in range(2):
            hand_on(part, piece).wait_recv()

    def sides(ref, count):
        parts = [
            ref[piece, part * rows : (part + 1) * rows, :]
            for piece in range(count)
            for part in range(2)
        ]
        return jnp.concatenate(parts, axis=1)

    full = sides(r.xex, X_PIECES).astype(F32)
    inv = lax.rsqrt(jnp.mean(full * full, axis=-1, keepdims=True) + EPSILON)
    r.normed[...] = (full * inv * r.gain[...].astype(F32)).astype(BF16)
    for piece in range(X_PIECES):
        start = 2 * piece * x_wide
        both = jnp.concatenate(
            [r.normed[:, start : start + x_wide], r.normed[:, start + x_wide : start + 2 * x_wide]],
            axis=0,
        )
        spread = dot(r.select[...], both).astype(BF16)
        r.dispx[piece] = spread.reshape(nz, 2 * cap, x_wide)
        pairs(
            lambda step, side, piece=piece: dispatch_x(piece, step, side).start(), 0, x_first
        )
        own_copies.append(
            pltpu.make_async_copy(
                r.dispx.at[piece, chip], r.xbuf.at[0, 1, piece], r.l_sem.at[len(own_copies)]
            )
        )
        own_copies[-1].start()

    same = iota((rows, rows), 0) == iota((rows, rows), 1)

    def upright(line):
        return jnp.sum(jnp.where(same, line, 0), axis=1, keepdims=True)

    expert_ids = iota((rows, nz), 1)
    picked = [upright(r.picks[k : k + 1, :]) for k in range(2)]
    target_of = [upright(targets[k]) for k in range(2)]
    logits = dot(r.normed[...], r.router_t[...], (1, 1))
    scores = [
        jnp.sum(jnp.where(expert_ids == picked[k], logits, 0.0), axis=1, keepdims=True)
        for k in range(2)
    ]
    gates = [1.0 / (1.0 + jnp.exp(scores[1 - k] - scores[k])) for k in range(2)]
    places = iota((rows, LANES), 1)
    place_of = [target_of[k] - picked[k] * (2 * cap) for k in range(2)]
    slot_gates = jnp.zeros((nz, LANES), F32)
    for k in range(2):
        onehot = jnp.where(named[k], 1.0, 0.0).astype(BF16)
        for piece in split(jnp.where(places == place_of[k], gates[k], 0.0)):
            slot_gates = slot_gates + dot(onehot, piece)
    r.gate_out[...] = slot_gates.reshape(nz, 1, LANES)
    pairs(lambda step, side: give_gates(step, side).start())
    r.gate_in[0, 1] = r.gate_out[chip]
    r.gain_sum[...] = jnp.zeros_like(r.gain_sum)
    across_slots = iota((rows, nz * 2 * cap), 1)
    for part in range(2):
        mix = jnp.where(across_slots == target_of[0] + part * cap, gates[0], 0.0)
        mix = mix + jnp.where(across_slots == target_of[1] + part * cap, gates[1], 0.0)
        r.weights[part * rows : (part + 1) * rows, :] = mix.astype(BF16)

    for copy in own_copies:
        copy.wait()
    for load in loads:
        load.wait()

    def pick_rows(value, part):
        return value.reshape(4, 2 * cap, half_width)[:, part * cap : (part + 1) * cap].reshape(
            4 * cap, half_width
        )

    def receive_g(step):
        for piece in range(G_PIECES):
            dispatch_g(piece, step, 0).wait_recv()
        forward_g(step, 0).start()

        @pl.when(step > 0)
        def _():
            for piece in range(G_PIECES):
                dispatch_g(piece, step, 1).wait_recv()

        forward_g(step, 1).start()

    def compute_g(step):
        for side in range(2):
            forward_g(step, side).wait_recv()
        total = jnp.zeros((4 * cap, half_width), F32)
        for piece in range(G_PIECES):
            block = r.gbuf[step, :, piece].reshape(8 * cap, g_wide)
            for part in range(2):
                start = (2 * piece + part) * g_wide
                down = r.down_w[:, start : start + g_wide]
                total = total + pick_rows(dot(block, down, (1, 1)), part)
        r.hidden_grad[step] = total

    def receive_x(step):
        for piece in range(X_PIECES):
            dispatch_x(piece, step, 0).wait_recv()
        forward_x(step, 0).start()

        @pl.when(step > 0)
        def _():
            for piece in range(X_PIECES):
                dispatch_x(piece, step, 1).wait_recv()

        forward_x(step, 1).start()

    diagonal = iota((cap, LANES), 0) == iota((cap, LANES), 1)

    def compute_x(step):
        for side in range(2):
            forward_x(step, side).wait_recv()
        gate_pre = jnp.zeros((4 * cap, half_width), F32)
        up_pre = jnp.zeros((4 * cap, half_width), F32)
        for piece in range(X_PIECES):
            block = r.xbuf[step, :, piece].reshape(8 * cap, x_wide)
            for part in range(2):
                start = (2 * piece + part) * x_wide
                columns = slice(start, start + x_wide)
                gate_pre = gate_pre + pick_rows(dot(block, r.gate_w[columns, :]), part)
                up_pre = up_pre + pick_rows(dot(block, r.up_w[columns, :]), part)
        hidden_grad = r.hidden_grad[step]
        logistic = jax.nn.sigmoid(gate_pre)
        activated = gate_pre * logistic
        share = jnp.sum(activated * up_pre * hidden_grad, axis=1, keepdims=True)
        for which in range(4):
            column = share[which * cap : (which + 1) * cap]
            line = jnp.sum(jnp.where(diagonal, column, 0.0), axis=0, keepdims=True)
            if which < 2:
                r.own_share[step, which] = line
            else:
                r.share_send[step, which - 2] = line
        partial_share(step).start()
        gate_grad = (
            hidden_grad * up_pre * logistic * (1.0 + gate_pre * (1.0 - logistic))
        ).astype(BF16)
        up_grad = (hidden_grad * activated).astype(BF16)
        chunk = min(512, width)
        for start in range(0, width, chunk):
            columns = slice(start, start + chunk)
            back = dot(gate_grad, r.gate_w[columns, :], (1, 1)) + dot(
                up_grad, r.up_w[columns, :], (1, 1)
            )
            r.own[step, :, columns] = back[: 2 * cap]
            r.psend[step, :, columns] = back[2 * cap :].astype(BF16)
        partial(step).start()

    def finish(step):
        partial_share(step).wait_recv()
        for side in range(2):
            r.ssend[step, side] = r.own_share[step, side] + r.share_recv[step, side]
        give_share(step, 0).start()

        @pl.when(step > 0)
        def _():
            give_share(step, 1).start()

        partial(step).wait_recv()
        total = r.own[step] + r.precv[step].astype(F32)
        stacked = []
        for side in range(2):
            mine = total[side * cap : (side + 1) * cap]
            stacked.append(jnp.concatenate([mine[:, :half_model], mine[:, half_model:]], axis=0))
            r.rsend[step, side] = stacked[side].astype(BF16)
        @pl.when(step < r_first)
        def _():
            give_back(step, 0).start()

        @pl.when((step > 0) & (step < r_first))
        def _():
            give_back(step, 1).start()

        give_gates(step, 0).wait_recv()

        @pl.when(step > 0)
        def _():
            give_gates(step, 1).wait_recv()

        for side in range(2):
            line = r.gate_in[step, side]
            column = jnp.sum(jnp.where(diagonal, line, 0.0), axis=1, keepdims=True)
            term = stacked[side] * r.xbuf[step, side, 0].astype(F32)
            for part in range(2):
                r.gain_sum[part : part + 1, :] += jnp.sum(
                    term[part * cap : (part + 1) * cap] * column, axis=0, keepdims=True
                )

    def pipeline_g(turn, carry):
        @pl.when(turn < steps)
        def _():
            receive_g(turn)

        @pl.when(turn >= 1)
        def _():
            compute_g(turn - 1)

        return carry

    def pipeline_x(turn, carry):
        @pl.when(turn < steps)
        def _():
            receive_x(turn)

        @pl.when(turn < steps - x_first)
        def _():
            for piece in range(X_PIECES):
                for side in range(2):
                    dispatch_x(piece, turn + x_first, side).start()

        @pl.when((turn >= 1) & (turn <= steps))
        def _():
            compute_x(turn - 1)

        @pl.when(turn >= 2)
        def _():
            finish(turn - 2)

        return carry

    lax.fori_loop(0, steps + 1, pipeline_g, 0)
    lax.fori_loop(0, steps + 2, pipeline_x, 0)

    base = G_PIECES + X_PIECES
    self_back = pltpu.make_async_copy(r.rsend.at[0, 1], r.ret.at[chip], r.l_sem.at[base])
    self_share = pltpu.make_async_copy(r.ssend.at[0, 1], r.sret.at[chip], r.l_sem.at[base + 1])
    self_back.start()
    self_share.start()
    for block in range(blocks):
        part, column = divmod(block * LANES, half_model)
        r.y_src[block : block + 1, :] = r.gain_sum[part : part + 1, column : column + LANES]
    across_gain = remote(r.y_src, r.y_dst, (r.x_send, r.x_recv), 1, sibling)
    across_gain.start()
    self_share.wait()
    pairs(lambda step, side: give_share(step, side).wait_recv())

    shares = r.sret[...].reshape(nz, LANES)
    first, second = split(shares)
    third = (shares - first.astype(F32) - second.astype(F32)).astype(BF16)
    gate_share = []
    for k in range(2):
        onehot = jnp.where(expert_ids == picked[k], 1.0, 0.0).astype(BF16)
        line = dot(onehot, first) + dot(onehot, second) + dot(onehot, third)
        gate_share.append(
            jnp.sum(jnp.where(places == place_of[k], line, 0.0), axis=1, keepdims=True)
        )
    mean_share = gates[0] * gate_share[0] + gates[1] * gate_share[1]
    logit_grad = jnp.zeros((rows, nz), F32)
    for k in range(2):
        select_grad = gates[k] * (gate_share[k] - mean_share)
        logit_grad = logit_grad + jnp.where(expert_ids == picked[k], select_grad, 0.0)
    grad_high, grad_low = split(logit_grad)
    router_term = dot(grad_high, r.normed[...], (0, 0)) + dot(grad_low, r.normed[...], (0, 0))
    for block in range(blocks):
        r.stage[:, block, :] = router_term[:, block * LANES : (block + 1) * LANES]
    r.q_src[...] = r.stage[...].astype(BF16)
    others(lambda offset: reduce_router(offset).start())
    pairs(lambda step, side: give_back(step, side).start(), r_first, r_second)
    self_reduce = pltpu.make_async_copy(r.q_src.at[chip], r.q_dst.at[0], r.l_sem.at[base + 2])
    self_reduce.start()
    router_part = dot(grad_high, r.router_t[...]) + dot(grad_low, r.router_t[...])

    self_reduce.wait()
    others(lambda offset: reduce_router(offset).wait_recv())
    r.x_src[...] = jnp.sum(r.q_dst[...].astype(F32), axis=0)
    across_router = remote(r.x_src, r.x_dst, (r.x_send, r.x_recv), 0, sibling)
    across_router.start()

    across_gain.wait_recv()
    across_router.wait_recv()
    router_row = r.x_src[...] + r.x_dst[...]
    gain_row = r.y_src[...] + r.y_dst[...]
    mine = lax.rem(chip, 2) == core
    r.a_src[...] = jnp.where(mine, router_row, gain_row).astype(BF16)
    others(lambda offset: gather_router(offset).start())
    r.a_dst[chip] = r.a_src[...]

    pairs(lambda step, side: give_back(step, side).start(), r_second, steps)
    self_back.wait()
    pairs(lambda step, side: give_back(step, side).wait_recv())
    came_back = r.ret[...].reshape(nz * 2 * cap, half_model)
    both = dot(r.weights[...], came_back)
    normed_grad = jnp.concatenate([both[:rows], both[rows:]], axis=1) + router_part

    unit = sides(r.xex, X_PIECES).astype(F32) * inv
    scaled = normed_grad * r.gain[...].astype(F32)
    mean_scaled = jnp.mean(scaled * unit, axis=-1, keepdims=True)
    returned = sides(r.gex, G_PIECES).astype(F32)
    r.lig[...] = (returned + inv * (scaled - unit * mean_scaled)).astype(BF16)

    others(lambda offset: gather_router(offset).wait_recv())
    swap = remote(r.a_dst, r.b_dst, (r.x_send, r.x_recv), 2, sibling)
    swap.start()

    for piece in range(G_PIECES):
        for part in range(2):
            hand_back(part, piece).wait_send()
        pairs(lambda step, side, piece=piece: dispatch_g(piece, step, side).wait_send())
    for piece in range(X_PIECES):
        for part in range(2):
            hand_on(part, piece).wait_send()
        pairs(lambda step, side, piece=piece: dispatch_x(piece, step, side).wait_send())

    def drain(step, carry):
        for side in range(2):
            forward_g(step, side).wait_send()
            forward_x(step, side).wait_send()
        partial(step).wait_send()
        partial_share(step).wait_send()
        return carry

    lax.fori_loop(0, steps, drain, 0)
    pairs(lambda step, side: give_back(step, side).wait_send())
    pairs(lambda step, side: give_share(step, side).wait_send())
    others(lambda offset: reduce_router(offset).wait_send())
    others(lambda offset: gather_router(offset).wait_send())
    pairs(lambda step, side: give_gates(step, side).wait_send())
    across_router.wait_send()
    across_gain.wait_send()

    swap.wait()
    here = r.a_dst[...].astype(F32)
    there = r.b_dst[...].astype(F32)
    tall = here.shape[1]
    is_here = lax.rem(iota((nz, tall, LANES), 0), 2) == core
    router_rows = jnp.where(is_here, here, there)
    gain_rows = jnp.sum(jnp.where(is_here, there, here), axis=0)
    for block in range(blocks):
        columns = slice(block * LANES, (block + 1) * LANES)
        total = router_rows[:, block, :]
        r.router_total[:, columns] = total
        from_router = jnp.sum(total * r.router_t[:, columns].astype(F32), axis=0, keepdims=True)
        r.gain_total[:, columns] = (gain_rows[block : block + 1, :] + from_router) / r.gain[
            :, columns
        ].astype(F32)


def exchange(nz, cap, sections, lengths, picks, gain, router_t, acts, cots, gate, up, down):
    steps = nz // 2
    rows, width = acts.shape[1:]
    half_width = gate.shape[1]
    half_model = width // 2
    lines = width // LANES
    g_wide = half_model // G_PIECES
    x_wide = half_model // X_PIECES
    vmem = pl.BlockSpec(memory_space=pltpu.VMEM)
    anywhere = pl.BlockSpec(memory_space=pl.ANY)

    def sems(*shape):
        return pltpu.SemaphoreType.DMA(shape)

    tall = -(-lines // 16) * 16
    scratch = {
        "gate_w": pltpu.VMEM((width, half_width), BF16),
        "up_w": pltpu.VMEM((width, half_width), BF16),
        "down_w": pltpu.VMEM((half_width, width), BF16),
        "select": pltpu.VMEM((nz * 2 * cap, 2 * rows), BF16),
        "gex": pltpu.VMEM((G_PIECES, 2 * rows, g_wide), BF16),
        "xex": pltpu.VMEM((X_PIECES, 2 * rows, x_wide), BF16),
        "normed": pltpu.VMEM((rows, width), BF16),
        "dispg": pltpu.VMEM((G_PIECES, nz, 2 * cap, g_wide), BF16),
        "dispx": pltpu.VMEM((X_PIECES, nz, 2 * cap, x_wide), BF16),
        "gbuf": pltpu.VMEM((steps, 4, G_PIECES, 2 * cap, g_wide), BF16),
        "xbuf": pltpu.VMEM((steps, 4, X_PIECES, 2 * cap, x_wide), BF16),
        "hidden_grad": pltpu.VMEM((steps, 4 * cap, half_width), F32),
        "own": pltpu.VMEM((steps, 2 * cap, width), F32),
        "psend": pltpu.VMEM((steps, 2 * cap, width), BF16),
        "precv": pltpu.VMEM((steps, 2 * cap, width), BF16),
        "own_share": pltpu.VMEM((steps, 2, 1, LANES), F32),
        "share_send": pltpu.VMEM((steps, 2, 1, LANES), F32),
        "share_recv": pltpu.VMEM((steps, 2, 1, LANES), F32),
        "rsend": pltpu.VMEM((steps, 2, 2 * cap, half_model), BF16),
        "ret": pltpu.VMEM((nz, 2 * cap, half_model), BF16),
        "ssend": pltpu.VMEM((steps, 2, 1, LANES), F32),
        "sret": pltpu.VMEM((nz, 1, LANES), F32),
        "gate_out": pltpu.VMEM((nz, 1, LANES), F32),
        "gate_in": pltpu.VMEM((steps, 2, 1, LANES), F32),
        "gain_sum": pltpu.VMEM((2, half_model), F32),
        "weights": pltpu.VMEM((2 * rows, nz * 2 * cap), BF16),
        "stage": pltpu.VMEM((nz, tall, LANES), F32),
        "q_src": pltpu.VMEM((nz, tall, LANES), BF16),
        "q_dst": pltpu.VMEM((nz, tall, LANES), BF16),
        "x_src": pltpu.VMEM((tall, LANES), F32),
        "x_dst": pltpu.VMEM((tall, LANES), F32),
        "y_src": pltpu.VMEM((tall, LANES), F32),
        "y_dst": pltpu.VMEM((tall, LANES), F32),
        "a_src": pltpu.VMEM((tall, LANES), BF16),
        "a_dst": pltpu.VMEM((nz, tall, LANES), BF16),
        "b_dst": pltpu.VMEM((nz, tall, LANES), BF16),
        "w_sem": sems(3),
        "l_sem": sems(G_PIECES + X_PIECES + 3),
        "ge_send": sems(2 * G_PIECES),
        "ge_recv": sems(2 * G_PIECES),
        "xe_send": sems(2 * X_PIECES),
        "xe_recv": sems(2 * X_PIECES),
        "gd_send": sems(G_PIECES, steps, 2),
        "gd_recv": sems(G_PIECES, steps, 2),
        "xd_send": sems(X_PIECES, steps, 2),
        "xd_recv": sems(X_PIECES, steps, 2),
        "gf_send": sems(steps, 2),
        "gf_recv": sems(steps, 2),
        "xf_send": sems(steps, 2),
        "xf_recv": sems(steps, 2),
        "p_send": sems(steps),
        "p_recv": sems(steps),
        "h_send": sems(steps),
        "h_recv": sems(steps),
        "r_send": sems(steps, 2),
        "r_recv": sems(steps, 2),
        "s_send": sems(steps, 2),
        "s_recv": sems(steps, 2),
        "q_send": sems(nz),
        "q_recv": sems(nz),
        "x_send": sems(3),
        "x_recv": sems(3),
        "gg_send": sems(steps, 2),
        "gg_recv": sems(steps, 2),
        "a_send": sems(nz),
        "a_recv": sems(nz),
    }
    operands = ["lengths", "picks", "gain", "router_t", "acts", "cots"]
    operands += ["gate_hbm", "up_hbm", "down_hbm"]
    names = operands + ["lig", "router_total", "gain_total"] + list(scratch)
    return pl.pallas_call(
        functools.partial(kernel, nz, cap, sections, names),
        out_shape=(
            jax.ShapeDtypeStruct((rows, width), BF16),
            jax.ShapeDtypeStruct((nz, width), F32),
            jax.ShapeDtypeStruct((1, width), F32),
        ),
        in_specs=[vmem] * 4 + [anywhere] * 5,
        out_specs=(vmem, vmem, vmem),
        scratch_shapes=list(scratch.values()),
        compiler_params=pltpu.CompilerParams(
            collective_id=0, has_side_effects=True, vmem_limit_bytes=44 * 1024 * 1024
        ),
        cost_estimate=pl.CostEstimate(
            flops=8_000_000_000, bytes_accessed=8_000_000, transcendentals=200_000
        ),
    )(lengths, picks, gain, router_t, acts, cots, gate, up, down)


def per_device(
    activations,
    cotangents,
    norm_gain,
    routes,
    lengths,
    router_weight,
    gate_weight,
    up_weight,
    down_weight,
):
    rows, width = activations.shape[1:]
    experts = router_weight.shape[2]
    top = routes.shape[2]
    cap = 3 * rows * top // (2 * experts)
    lig, router_total, gain_total = exchange(
        experts,
        cap,
        lax.axis_size("section"),
        lengths,
        routes[0].T,
        norm_gain,
        router_weight[0].T,
        activations,
        cotangents,
        gate_weight[0, 0],
        up_weight[0, 0],
        down_weight[0, 0],
    )
    return (lig[None], router_total.T[None], gain_total)


def solution(mesh):
    in_specs = (
        P("section", "expert", None),
        P("section", "expert", None),
        P("section", None),
        P("section", "expert", None),
        P("section", "expert"),
        P("section", None, None),
        P("section", "expert", None, None),
        P("section", "expert", None, None),
        P("section", "expert", None, None),
    )
    out_specs = (P("section", "expert", None), P("section", None, None), P("section", None))
    return jax.shard_map(
        per_device, mesh=mesh, in_specs=in_specs, out_specs=out_specs, check_vma=False
    )
```
